32 devices in a mesh: req: 16 (over z, y, x), mlp: 2 (over core).
Axes of the slice: x: 2, y: 2, z: 4, core: 2. Of those that a mesh axis runs over, the one named last changes fastest.
Arguments:
- q_in: bfloat16 [8192, 4096], P('req', 'mlp'), may hold values from -6 to 6
- kv_in: bfloat16 [2, 8192, 1024], P(None, 'req', 'mlp'), may hold values from -6 to 6
- prefix_kv: bfloat16 [2, 1024, 1024], P(None, 'req', 'mlp'), may hold values from -1 to 1
- hidden_in: bfloat16 [8192, 2560], P(('req', 'mlp')), may hold values from -0.625 to 0.625
- q_gain: float32 [128], replicated, may hold values from 0.5 to 2.5
- k_gain: float32 [128], replicated, may hold values from 0.5 to 2.5
- post_gain: float32 [2560], replicated, may hold values from 0.1 to 1.9
- w_out: bfloat16 [4096, 2560], P('mlp'), may hold values from -0.09375 to 0.09375
- w_gate: bfloat16 [2560, 5120], P('req', 'mlp'), may hold values from -0.125 to 0.125
- w_up: bfloat16 [2560, 5120], P('req', 'mlp'), may hold values from -0.125 to 0.125
- w_down_t: bfloat16 [2560, 5120], P('req', 'mlp'), may hold values from -0.078125 to 0.078125
- lengths: int32 [16, 8], P('req'), may hold values from 1 to 256, 512 in all within a row
- row_group: int32 [16], P('req'), may hold values from 0 to 1
- owner_block: int32 [16], replicated, may hold values from 0 to 15, each once
Outputs:
- hidden_out: bfloat16 [8192, 2560], P(('req', 'mlp'))
The draws below stay inside these ranges and needn't reach their ends.
Inputs may be any that keep to these rules, and one draw needn't show every extreme that they name: Each index's 8 lengths sum to 512; the largest is exactly 256. `owner_block`: A permutation; block b belongs to group b // 8, so every group has 8 blocks.
All inputs are finite; a program needn't handle non-finite values.
Results may differ from the reference program's by a relative error of at most 0.023.
Values may be sent and summed in bfloat16 or wider, within the bound.
No kernel may reach another device: no remote copies, remote signals or barrier semaphores. Data moves between devices by JAX's collectives and lax.ppermute only.
A program may use at most 128 MiB of HBM per device.

```python
import math
import jax
import jax.numpy as jnp
import numpy as np
from jax import lax

D = 2560
H = 32
KVH = 8
HD = 128
FF = 5120
TOK_ROW = 512
NRQ = 8
PB = 64
PLEN = 512
BPG = 8
NGRP = 2
TOKENS = 8192
PREFIX_ALL = 1024
N_REQ = 16


def touch_ends(values, own_key, smallest, top_value):
    longest = values.shape.index(max(values.shape))
    spots = []
    for shift in (0, 1):
        where = [jax.random.randint(jax.random.fold_in(own_key, axis), (), 0, length) for axis, length in enumerate(values.shape)]
        where[longest] = (where[longest] + shift) % values.shape[longest]
        spots.append(tuple(where))
    return values.at[spots[0]].set(smallest).at[spots[1]].set(top_value)


def steps_of(rng, shape, cuts, low, top_value):
    gain, own = 1.0, jax.random.fold_in(rng, 6)
    for position, parts in cuts:
        steps = jnp.exp(jax.random.uniform(jax.random.fold_in(own, position), (parts,), jnp.float32, low / len(cuts), top_value / len(cuts)))
        gain = gain * jnp.repeat(steps, shape[position] // parts).reshape([-1 if axis == position else 1 for axis in range(len(shape))])
    return gain


def profile(number_of, total, most, skew):
    portions = [(1 << 20) // math.isqrt(grade ** skew) + 1 for grade in range(2, number_of + 1)]
    surplus, holding = total - most - (number_of - 1), [1] * (number_of - 1)
    while surplus > 0:
        movable = [i for i in range(number_of - 1) if holding[i] < most]
        pool, remaining = sum([portions[i] for i in movable]), surplus
        for i in movable:
            extra = min(most - holding[i], max(1, remaining * portions[i] // pool), surplus)
            holding[i] = holding[i] + extra
            surplus = surplus - extra
    return np.array([most] + holding)


def uneven(stream_key, amount, total, limit, skew):
    if amount == 2:
        one = jax.random.randint(stream_key, (), max(1, total - limit), min(limit, total - 1) + 1)
        return jnp.stack([one, total - one])
    tallies = jnp.asarray(profile(amount, total, limit, skew), jnp.int32)
    twos = (amount - 1) // 2
    donor, taker = tallies[1:1 + 2 * twos:2], tallies[2:2 + 2 * twos:2]
    margin = jnp.minimum(donor - 1, limit - taker)
    shifted = jax.random.randint(jax.random.fold_in(stream_key, 1), (twos,), 0, 1 << 20) % (margin + 1)
    tallies = tallies.at[1:1 + 2 * twos:2].set(donor - shifted).at[2:2 + 2 * twos:2].set(taker + shifted)
    return tallies[jax.random.permutation(jax.random.fold_in(stream_key, 2), amount)]


def noise(stream_key, extent, spread, reach, shards=(), kind=jnp.bfloat16):
    values = jax.random.normal(stream_key, extent, jnp.float32) * spread
    if len(shards) > 0:
        values = steps_of(stream_key, extent, shards, -0.22, 0.18) * values
    return jnp.clip(values, min=-reach, max=reach).astype(kind)


def setup_inputs(seed: int = 0) -> dict:
    arg_keys = jax.random.split(jax.random.key(seed), 15)
    q_in = noise(arg_keys[0], (TOKENS, H * HD), 1.0, 6.0, ((0, 16), (1, 2)))
    kv_in = noise(arg_keys[1], (2, TOKENS, KVH * HD), 1.0, 6.0, ((1, 16), (2, 2)))
    prefix_kv = jnp.clip(jax.random.uniform(arg_keys[2], (2, PREFIX_ALL, KVH * HD), jnp.float32, -1.0, 1.0) * steps_of(arg_keys[2], (2, PREFIX_ALL, KVH * HD), ((1, 16), (2, 2)), -0.4, 0.0), -1.0, 1.0).astype(jnp.bfloat16)
    hidden_in = noise(arg_keys[3], (TOKENS, D), 0.1, 0.625, ((0, 32),))
    q_gain = jnp.clip(jnp.exp(jax.random.uniform(arg_keys[4], (HD,), jnp.float32, math.log(0.5), math.log(2.5))), 0.5, 2.5)
    k_gain = jnp.clip(jnp.exp(jax.random.uniform(arg_keys[5], (HD,), jnp.float32, math.log(0.5), math.log(2.5))), 0.5, 2.5)
    post_gain = jnp.clip(1.0 + 0.18 * jax.random.normal(arg_keys[6], (D,), jnp.float32), 0.1, 1.9)
    w_out = noise(arg_keys[7], (H * HD, D), (H * HD) ** -0.5, 0.09375, ((0, 2),))
    w_gate = noise(arg_keys[8], (D, FF), D ** -0.5, 0.125, ((0, 16), (1, 2)))
    w_up = noise(arg_keys[9], (D, FF), D ** -0.5, 0.125, ((0, 16), (1, 2)))
    w_down_t = noise(arg_keys[10], (D, FF), FF ** -0.5, 0.078125, ((0, 16), (1, 2)))
    lengths = jax.vmap(lambda own: uneven(own, NRQ, TOK_ROW, TOK_ROW // 2, 2))(jax.random.split(arg_keys[11], N_REQ)).reshape((N_REQ, NRQ)).astype(jnp.int32)
    row_group = touch_ends(jax.random.randint(arg_keys[12], (N_REQ,), 0, NGRP), jax.random.fold_in(arg_keys[12], 1), 0, NGRP - 1).astype(jnp.int32)
    owner_block = jax.random.permutation(arg_keys[13], PREFIX_ALL // PB).astype(jnp.int32)
    return dict(q_in=q_in, kv_in=kv_in, prefix_kv=prefix_kv, hidden_in=hidden_in, q_gain=q_gain, k_gain=k_gain, post_gain=post_gain, w_out=w_out, w_gate=w_gate, w_up=w_up, w_down_t=w_down_t, lengths=lengths, row_group=row_group, owner_block=owner_block)


EPSILON = 1e-06
THETA = 1000000.0

def rms_scale(values, gains):
    mean_sq = lax.optimization_barrier(jnp.mean(values * values, axis=-1, keepdims=True))
    return values * lax.rsqrt(mean_sq + EPSILON) * gains

def rotate(values, positions):
    half_width = values.shape[-1] // 2
    exponent = jnp.arange(half_width, dtype=jnp.float32) * (2.0 / values.shape[-1])
    inv_freq = jnp.power(jnp.float32(THETA), -exponent)
    angles = positions.astype(jnp.float32)[:, None] * inv_freq[None, :]
    cosine = jnp.cos(angles)[:, None, :]
    sine_part = jnp.sin(angles)[:, None, :]
    first_half = values[..., :half_width]
    second = values[..., half_width:]
    return jnp.concatenate([first_half * cosine - second * sine_part, second * cosine + first_half * sine_part], axis=-1)

def slot_layout(row_lengths, tok_count):
    row_lengths = row_lengths.astype(jnp.int32)
    req_ends = jnp.cumsum(row_lengths).astype(jnp.int32)
    starts = req_ends - row_lengths
    slot_ids = jnp.arange(tok_count, dtype=jnp.int32)
    request = lax.optimization_barrier(jnp.sum((slot_ids[:, None] >= req_ends[None, :]).astype(jnp.int32), axis=1)).astype(jnp.int32)
    member = request[:, None] == jnp.arange(row_lengths.shape[0], dtype=jnp.int32)[None, :]
    offset = slot_ids - lax.optimization_barrier(jnp.sum(jnp.where(member, starts[None, :], 0), axis=1)).astype(jnp.int32)
    return (request, offset)

def attention(queries, pre_keys, pre_vals, suffix_key_rows, suffix_value_rows, allowed):
    tok_count, head_count, head_width = queries.shape
    groups = pre_keys.shape[1]
    grouped_heads = queries.astype(jnp.float32).reshape(tok_count, groups, head_count // groups, head_width)
    logit_scale = 1.0 / math.sqrt(head_width)
    pre_weights = jnp.exp(jnp.einsum('tgrd,pgd->grtp', grouped_heads, pre_keys.astype(jnp.float32)) * logit_scale)
    suffix_logits = jnp.einsum('fknp,bkp->knfb', grouped_heads, suffix_key_rows.astype(jnp.float32)) * logit_scale
    suf_weights = jnp.where(allowed[None, None, :, :], jnp.exp(suffix_logits), 0.0)
    total = lax.optimization_barrier(jnp.sum(pre_weights, axis=-1)) + lax.optimization_barrier(jnp.sum(suf_weights, axis=-1))
    pre_round = lax.optimization_barrier(pre_weights.astype(jnp.bfloat16)).astype(jnp.float32)
    suffix_rounding = lax.optimization_barrier(suf_weights.astype(jnp.bfloat16)).astype(jnp.float32)
    numerator = jnp.einsum('grtp,pgd->grtd', pre_round, pre_vals.astype(jnp.float32))
    numerator = numerator + jnp.einsum('mabi,ime->mabe', suffix_rounding, suffix_value_rows.astype(jnp.float32))
    result = numerator / total[..., None]
    return jnp.transpose(result, (2, 0, 1, 3)).reshape(tok_count, head_count * head_width).astype(jnp.bfloat16)

def reference(q_in, kv_in, prefix_kv, hidden_in, q_gain, k_gain, post_gain, w_out, w_gate, w_up, w_down_t, lengths, row_group, owner_block):
    inverse = jnp.argsort(owner_block).astype(jnp.int32)
    prefix_blocks = prefix_kv.reshape(2, N_REQ, PB, KVH * HD)

    def one_row(row_index):
        first_token = row_index * TOK_ROW
        row_queries = lax.dynamic_slice_in_dim(q_in, first_token, TOK_ROW, 0)
        row_kv = lax.dynamic_slice_in_dim(kv_in, first_token, TOK_ROW, 1)
        row_hidden = lax.dynamic_slice_in_dim(hidden_in, first_token, TOK_ROW, 0)
        request, offset = slot_layout(lengths[row_index], TOK_ROW)
        positions = offset + PLEN
        queries = rotate(rms_scale(row_queries.astype(jnp.float32).reshape(TOK_ROW, H, HD), q_gain), positions).astype(jnp.bfloat16)
        suffix_key_rows = rotate(rms_scale(row_kv[0].astype(jnp.float32).reshape(TOK_ROW, KVH, HD), k_gain), positions).astype(jnp.bfloat16)
        suffix_value_rows = row_kv[1].reshape(TOK_ROW, KVH, HD)
        picked = lax.dynamic_slice_in_dim(inverse, (row_group[row_index] * BPG).astype(jnp.int32), BPG, 0)
        chosen = jnp.take(prefix_blocks, picked, axis=1).reshape(2, PLEN, KVH, HD)
        slot_ids = jnp.arange(TOK_ROW, dtype=jnp.int32)
        allowed = (request[:, None] == request[None, :]) & (slot_ids[None, :] <= slot_ids[:, None])
        attn = attention(queries, chosen[0], chosen[1], suffix_key_rows, suffix_value_rows, allowed)
        projected = jnp.dot(attn, w_out, preferred_element_type=jnp.float32)
        resid = (row_hidden.astype(jnp.float32) + projected).astype(jnp.bfloat16)
        normed = rms_scale(resid.astype(jnp.float32), post_gain).astype(jnp.bfloat16)
        gate = jnp.dot(normed, w_gate, preferred_element_type=jnp.float32)
        upward = jnp.dot(normed, w_up, preferred_element_type=jnp.float32)
        act = (jax.nn.silu(gate) * upward).astype(jnp.bfloat16)
        down = lax.dot_general(act, w_down_t, (((1,), (1,)), ((), ())), preferred_element_type=jnp.float32)
        return (resid.astype(jnp.float32) + down).astype(jnp.bfloat16)
    rows_out = lax.map(one_row, jnp.arange(N_REQ, dtype=jnp.int32))
    return rows_out.reshape(TOKENS, D)
```

```python
import math

import jax
import jax.numpy as jnp
from jax import lax
from jax.sharding import PartitionSpec as P

HD = 128
PB = 64
PLEN = 512
BPG = 8
GROUP = 4


EPSILON = 1e-06
THETA = 1000000.0


def rms_scale(values, gains):
    mean_sq = jnp.mean(values * values, axis=-1, keepdims=True)
    return values * lax.rsqrt(mean_sq + EPSILON) * gains


def rotate(values, positions):
    half_width = values.shape[-1] // 2
    exponent = jnp.arange(half_width, dtype=jnp.float32) * (2.0 / values.shape[-1])
    inv_freq = jnp.power(jnp.float32(THETA), -exponent)
    angles = positions.astype(jnp.float32)[:, None] * inv_freq[None, :]
    cosine = jnp.cos(angles)[:, None, :]
    sine_part = jnp.sin(angles)[:, None, :]
    first_half = values[..., :half_width]
    second = values[..., half_width:]
    return jnp.concatenate(
        [first_half * cosine - second * sine_part, second * cosine + first_half * sine_part],
        axis=-1,
    )


def slot_layout(row_lengths, tok_count):
    req_ends = jnp.cumsum(row_lengths)
    starts = req_ends - row_lengths
    slot_ids = jnp.arange(tok_count, dtype=jnp.int32)
    request = jnp.sum((slot_ids[:, None] >= req_ends[None, :]).astype(jnp.int32), axis=1)
    member = request[:, None] == jnp.arange(row_lengths.shape[0], dtype=jnp.int32)[None, :]
    offset = slot_ids - jnp.sum(jnp.where(member, starts[None, :], 0), axis=1)
    return (request, offset)


def attention(queries, pre_keys, pre_vals, suffix_key_rows, suffix_value_rows, allowed):
    tok_count, head_count, head_width = queries.shape
    groups = pre_keys.shape[1]
    grouped_heads = queries.reshape(tok_count, groups, head_count // groups, head_width)
    logit_scale = 1.0 / math.sqrt(head_width)
    pre_weights = jnp.exp(
        jnp.einsum("tgrd,pgd->grtp", grouped_heads, pre_keys, preferred_element_type=jnp.float32)
        * logit_scale
    )
    suffix_logits = (
        jnp.einsum(
            "fknp,bkp->knfb", grouped_heads, suffix_key_rows, preferred_element_type=jnp.float32
        )
        * logit_scale
    )
    suf_weights = jnp.where(allowed[None, None, :, :], jnp.exp(suffix_logits), 0.0)
    total = jnp.sum(pre_weights, axis=-1) + jnp.sum(suf_weights, axis=-1)
    numerator = jnp.einsum(
        "grtp,pgd->grtd",
        pre_weights.astype(jnp.bfloat16),
        pre_vals,
        preferred_element_type=jnp.float32,
    )
    numerator = numerator + jnp.einsum(
        "mabi,ime->mabe",
        suf_weights.astype(jnp.bfloat16),
        suffix_value_rows,
        preferred_element_type=jnp.float32,
    )
    result = numerator / total[..., None]
    return (
        jnp.transpose(result, (2, 0, 1, 3))
        .reshape(tok_count, head_count * head_width)
        .astype(jnp.bfloat16)
    )


def activate(gate, upward):
    return (jax.nn.silu(gate) * upward).astype(jnp.bfloat16)


def swap(value, axis, size, bits):
    return lax.ppermute(value, axis, [(i, i ^ bits) for i in range(size)])


def per_device(
    q_in,
    kv_in,
    prefix_kv,
    hidden_in,
    q_gain,
    k_gain,
    post_gain,
    w_out,
    w_gate,
    w_up,
    w_down_t,
    lengths,
    row_group,
    owner_block,
):
    n_req, n_mlp = lax.axis_size("req"), lax.axis_size("mlp")
    me, core = lax.axis_index("req"), lax.axis_index("mlp")
    seat = me % GROUP
    tok_count = q_in.shape[0]
    local_heads = q_in.shape[1] // HD
    local_groups = kv_in.shape[2] // HD
    lines = [[line + GROUP * i for i in range(n_req // GROUP)] for line in range(GROUP)]

    def spread(block):
        width = block.shape[1] // GROUP
        parts = []
        for k in range(GROUP):
            part = lax.dynamic_slice_in_dim(block, (seat ^ k) * width, width, 1)
            parts.append(part if k == 0 else swap(part, "req", n_req, k))
        ordered = jnp.take(jnp.stack(parts), jnp.arange(GROUP) ^ seat, axis=0)
        rows = ordered.reshape(GROUP * block.shape[0], width)
        return lax.all_gather(rows, "req", axis_index_groups=lines, axis=0, tiled=True)

    def both(part):
        return [part] + [swap(part, "mlp", n_mlp, k) for k in range(1, n_mlp)]

    gate_w = spread(w_gate)
    up_w = spread(w_up)
    down_w = spread(w_down_t)

    held = prefix_kv[None]
    bit = GROUP
    while bit < n_req:
        held = jnp.concatenate([held, swap(held, "req", n_req, bit)], axis=0)
        bit *= 2
    held = jnp.stack([held] + [swap(held, "req", n_req, k) for k in range(1, GROUP)], axis=1)
    held = held.reshape(n_req, 2, PB, local_groups * HD)
    inverse = jnp.argsort(owner_block)
    picked = lax.dynamic_slice_in_dim(inverse, row_group[0] * BPG, BPG, 0)
    chosen = jnp.take(held, picked ^ me, axis=0)
    chosen = jnp.transpose(chosen, (1, 0, 2, 3)).reshape(2, PLEN, local_groups, HD)

    request, offset = slot_layout(lengths[0], tok_count)
    positions = offset + PLEN
    queries = rotate(
        rms_scale(q_in.astype(jnp.float32).reshape(tok_count, local_heads, HD), q_gain), positions
    ).astype(jnp.bfloat16)
    suffix_key_rows = rotate(
        rms_scale(kv_in[0].astype(jnp.float32).reshape(tok_count, local_groups, HD), k_gain),
        positions,
    ).astype(jnp.bfloat16)
    suffix_value_rows = kv_in[1].reshape(tok_count, local_groups, HD)
    slot_ids = jnp.arange(tok_count, dtype=jnp.int32)
    allowed = (request[:, None] == request[None, :]) & (slot_ids[None, :] <= slot_ids[:, None])
    attn = attention(queries, chosen[0], chosen[1], suffix_key_rows, suffix_value_rows, allowed)

    own_rows = hidden_in.shape[0]
    summed = hidden_in.astype(jnp.float32)
    for k in reversed(range(n_mlp)):
        rows = lax.dynamic_slice_in_dim(attn, (core ^ k) * own_rows, own_rows, 0)
        terms = jnp.dot(rows, w_out, preferred_element_type=jnp.float32)
        if k > 0:
            terms = swap(terms.astype(jnp.bfloat16), "mlp", n_mlp, k).astype(jnp.float32)
        summed = summed + terms
    resid = summed.astype(jnp.bfloat16)
    own_normed = rms_scale(resid.astype(jnp.float32), post_gain).astype(jnp.bfloat16)

    normed = jnp.concatenate(
        [own_normed] + [swap(own_normed, "req", n_req, k) for k in range(1, GROUP)], axis=0
    )
    terms = 0.0
    for gate_part, up_part, down_part in zip(both(gate_w), both(up_w), both(down_w)):
        gate = jnp.dot(normed, gate_part, preferred_element_type=jnp.float32)
        upward = jnp.dot(normed, up_part, preferred_element_type=jnp.float32)
        act = activate(gate, upward)
        terms = terms + lax.dot_general(
            act, down_part, (((1,), (1,)), ((), ())), preferred_element_type=jnp.float32
        )
    terms = terms.reshape(GROUP, own_rows, -1)
    mixed = terms[0]
    for k in range(1, GROUP):
        mixed = mixed + swap(terms[k].astype(jnp.bfloat16), "req", n_req, k).astype(jnp.float32)
    return (resid.astype(jnp.float32) + mixed).astype(jnp.bfloat16)


def solution(mesh):
    in_specs = (
        P("req", "mlp"),
        P(None, "req", "mlp"),
        P(None, "req", "mlp"),
        P(("req", "mlp"), None),
        P(),
        P(),
        P(),
        P("mlp", None),
        P("req", "mlp"),
        P("req", "mlp"),
        P("req", "mlp"),
        P("req", None),
        P("req"),
        P(),
    )
    out_specs = P(("req", "mlp"), None)
    return jax.shard_map(
        per_device, mesh=mesh, in_specs=in_specs, out_specs=out_specs, check_vma=False
    )
```

```python
import functools
import math

import jax
import jax.numpy as jnp
from jax import lax
from jax.experimental import pallas as pl
from jax.experimental.pallas import tpu as pltpu
from jax.sharding import PartitionSpec as P

HD = 128
PB = 64
PLEN = 512
BPG = 8
GROUP = 4
VMEM_LIMIT = 48 * 1024 * 1024


EPSILON = 1e-06
THETA = 1000000.0


def rotation(positions):
    half_width = HD // 2
    exponent = jnp.arange(half_width, dtype=jnp.float32) * (2.0 / HD)
    inv_freq = jnp.power(jnp.float32(THETA), -exponent)
    angles = positions.astype(jnp.float32)[:, None] * inv_freq[None, :]
    cosine, sine = jnp.cos(angles), jnp.sin(angles)
    return jnp.concatenate([cosine, cosine], axis=1), jnp.concatenate([-sine, sine], axis=1)


def slot_layout(row_lengths, tok_count):
    req_ends = jnp.cumsum(row_lengths)
    starts = req_ends - row_lengths
    slot_ids = jnp.arange(tok_count, dtype=jnp.int32)
    request = jnp.sum((slot_ids[:, None] >= req_ends[None, :]).astype(jnp.int32), axis=1)
    member = request[:, None] == jnp.arange(row_lengths.shape[0], dtype=jnp.int32)[None, :]
    offset = slot_ids - jnp.sum(jnp.where(member, starts[None, :], 0), axis=1)
    return (request, offset)


def dot_rows(left, right):
    return lax.dot_general(
        left, right, (((1,), (1,)), ((), ())), preferred_element_type=jnp.float32
    )


def attention_kernel(
    start_ref, cos_ref, sin_ref, q_gain, k_gain, q_ref, k_ref, v_ref, pk_ref, pv_ref, out_ref, bias
):
    tok_count = k_ref.shape[1]
    tile = min(256, tok_count)
    scale = math.log2(math.e) / math.sqrt(HD)

    @pl.when(pl.program_id(0) == 0)
    def _():
        keys = lax.broadcasted_iota(jnp.int32, (tok_count, tok_count), 1)
        slots = lax.broadcasted_iota(jnp.int32, (tok_count, tok_count), 0)
        seen = (keys >= start_ref[...]) & (keys <= slots)
        bias[...] = jnp.where(seen, 0.0, -1e30)

    def prepare(values, gain, rows):
        values = values.astype(jnp.float32)
        mean_sq = jnp.mean(values * values, axis=-1, keepdims=True)
        scaled = values * lax.rsqrt(mean_sq + EPSILON) * gain[...]
        turned = scaled * cos_ref[rows, :] + pltpu.roll(scaled, HD // 2, 1) * sin_ref[rows, :]
        return turned.astype(jnp.bfloat16)

    key = prepare(k_ref[0], k_gain, pl.ds(0, tok_count))
    value = v_ref[0]
    pre_key = pk_ref[...].reshape(-1, HD)
    pre_value = pv_ref[...].reshape(-1, HD)
    for head in range(q_ref.shape[1] // HD):
        lanes = pl.ds(head * HD, HD)
        for first in range(0, tok_count, tile):
            rows = pl.ds(first, tile)
            last = first + tile
            query = prepare(q_ref[rows, lanes], q_gain, rows)
            pre_w = jnp.exp2(dot_rows(query, pre_key) * scale)
            suf_w = jnp.exp2(dot_rows(query, key[:last]) * scale + bias[rows, :last])
            total = jnp.sum(pre_w, axis=-1, keepdims=True) + jnp.sum(suf_w, axis=-1, keepdims=True)
            top = jnp.dot(
                pre_w.astype(jnp.bfloat16), pre_value, preferred_element_type=jnp.float32
            ) + jnp.dot(
                suf_w.astype(jnp.bfloat16), value[:last], preferred_element_type=jnp.float32
            )
            out_ref[rows, lanes] = (top / total).astype(out_ref.dtype)


def attention(start, cosine, sine, q_gain, k_gain, q_in, kv_in, chosen, first, count):
    tok_count = q_in.shape[0]
    groups = kv_in.shape[2] // HD
    width = q_in.shape[1] // groups
    blocks = chosen.shape[0]

    def same(rows, columns):
        return pl.BlockSpec((rows, columns), lambda g: (0, 0))

    def suffix(which):
        return pl.BlockSpec((1, tok_count, HD), lambda g: (which, 0, g + first))

    def prefix(which):
        return pl.BlockSpec((blocks, 1, PB, HD), lambda g: (0, which, 0, g + first))

    keys = tok_count + PLEN
    return pl.pallas_call(
        attention_kernel,
        grid=(count,),
        in_specs=[
            same(tok_count, 1),
            same(tok_count, HD),
            same(tok_count, HD),
            same(1, HD),
            same(1, HD),
            pl.BlockSpec((tok_count, width), lambda g: (0, g + first)),
            suffix(0),
            suffix(1),
            prefix(0),
            prefix(1),
        ],
        out_specs=pl.BlockSpec((tok_count, width), lambda g: (0, g)),
        out_shape=jax.ShapeDtypeStruct((tok_count, count * width), jnp.bfloat16),
        scratch_shapes=[pltpu.VMEM((tok_count, tok_count), jnp.float32)],
        compiler_params=pltpu.CompilerParams(vmem_limit_bytes=VMEM_LIMIT),
        cost_estimate=pl.CostEstimate(
            flops=4 * tok_count * keys * width * count,
            bytes_accessed=4 * tok_count * width * count,
            transcendentals=tok_count * keys * width // HD * count,
        ),
        name="attention",
    )(start, cosine, sine, q_gain, k_gain, q_in, kv_in, kv_in, chosen, chosen)


def project_kernel(core, *refs, n_parts, n_mlp):
    parts, weights, outs = refs[:n_parts], refs[n_parts : 2 * n_parts], refs[2 * n_parts :]
    rows = outs[0].shape[0]
    for k in range(n_mlp - 1, -1, -1):
        part = pl.ds(pl.multiple_of((core[0] ^ k) * rows, rows), rows)
        total = 0.0
        for x, w in zip(parts, weights):
            total = total + jnp.dot(x[part, :], w[...], preferred_element_type=jnp.float32)
        outs[k][...] = total.astype(outs[k].dtype)


def project(core, parts, w_out, n_mlp):
    tok_count, depth = parts[0].shape
    columns = w_out.shape[1]
    rows, tile = tok_count // n_mlp, 512
    n_parts = len(parts)
    return pl.pallas_call(
        functools.partial(project_kernel, n_parts=n_parts, n_mlp=n_mlp),
        grid_spec=pltpu.PrefetchScalarGridSpec(
            num_scalar_prefetch=1,
            grid=(columns // tile,),
            in_specs=[pl.BlockSpec((tok_count, depth), lambda n, core: (0, 0))] * n_parts
            + [
                pl.BlockSpec((depth, tile), functools.partial(lambda i, n, core: (i, n), i))
                for i in range(n_parts)
            ],
            out_specs=[pl.BlockSpec((rows, tile), lambda n, core: (0, n))] * n_mlp,
        ),
        out_shape=[
            jax.ShapeDtypeStruct((rows, columns), jnp.bfloat16 if k else jnp.float32)
            for k in range(n_mlp)
        ],
        compiler_params=pltpu.CompilerParams(vmem_limit_bytes=VMEM_LIMIT),
        cost_estimate=pl.CostEstimate(
            flops=2 * tok_count * depth * n_parts * columns,
            bytes_accessed=2 * depth * n_parts * (tok_count + columns) + 3 * tok_count * columns,
            transcendentals=0,
        ),
        name="project",
    )(core, *parts, *[w_out] * n_parts)


def normalize_kernel(hidden, gain, own, *refs):
    parts, resid_ref, normed_ref = refs[:-2], refs[-2], refs[-1]
    total = hidden[...].astype(jnp.float32) + own[...]
    for part in parts:
        total = total + part[...].astype(jnp.float32)
    resid = total.astype(resid_ref.dtype)
    resid_ref[...] = resid
    values = resid.astype(jnp.float32)
    mean_sq = jnp.mean(values * values, axis=-1, keepdims=True)
    normed = values * lax.rsqrt(mean_sq + EPSILON) * gain[...]
    normed_ref[...] = normed.astype(normed_ref.dtype)


def normalize(hidden, gain, own, parts):
    rows, columns = hidden.shape
    tile = min(64, rows)
    spec = pl.BlockSpec((tile, columns), lambda i: (i, 0))
    return pl.pallas_call(
        normalize_kernel,
        grid=(rows // tile,),
        in_specs=[spec, pl.BlockSpec((1, columns), lambda i: (0, 0)), spec] + [spec] * len(parts),
        out_specs=[spec, spec],
        out_shape=[jax.ShapeDtypeStruct(hidden.shape, hidden.dtype)] * 2,
        compiler_params=pltpu.CompilerParams(vmem_limit_bytes=VMEM_LIMIT),
        cost_estimate=pl.CostEstimate(
            flops=rows * columns * 8, bytes_accessed=rows * columns * 12, transcendentals=rows
        ),
        name="normalize",
    )(hidden, gain, own, *parts)


def gate_up_kernel(pair, *refs):
    x_refs, w_refs, refs = refs[:GROUP], refs[GROUP : GROUP + 4], refs[GROUP + 4 :]
    act_ref, x_all, weight, gate_sum, up_sum, sems = refs
    width = act_ref.shape[1]
    rows, depth = x_refs[0].shape
    half = depth // 2
    packed = len(weight.shape) == 3
    x_copies = [
        pltpu.make_async_copy(x_ref, x_all.at[i], sems.at[i]) for i, x_ref in enumerate(x_refs)
    ]
    w_copies = []
    for i, w_ref in enumerate(w_refs):
        which, kind = i // 2, i % 2
        if packed:
            place = weight.at[which, :, pl.ds(kind * width, width)]
        else:
            place = weight.at[which, kind]
        w_copies.append(pltpu.make_async_copy(w_ref, place, sems.at[GROUP + i]))
    for copy in w_copies[:2] + x_copies + w_copies[2:]:
        copy.start()
    for copy in w_copies[:2] + x_copies:
        copy.wait()
    for which in range(2):
        start = pair[0] if which == 0 else 1 - pair[0]
        columns = pl.ds(pl.multiple_of(start * half, 128), half)
        if which == 1:
            for copy in w_copies[2:]:
                copy.wait()

        def step(i, carry):
            x = x_all[i, :, columns]
            if packed:
                terms = jnp.dot(x, weight[which], preferred_element_type=jnp.float32)
                gate, upward = terms[:, :width], terms[:, width:]
            else:
                gate = jnp.dot(x, weight[which, 0], preferred_element_type=jnp.float32)
                upward = jnp.dot(x, weight[which, 1], preferred_element_type=jnp.float32)
            if which == 0:
                gate_sum[i] = gate
                up_sum[i] = upward
            else:
                gate = gate + gate_sum[i]
                upward = upward + up_sum[i]
                here = pl.ds(pl.multiple_of(i * rows, rows), rows)
                act_ref[here, :] = (gate / (1.0 + jnp.exp(-gate)) * upward).astype(act_ref.dtype)
            return carry

        lax.fori_loop(0, GROUP, step, 0)


def gate_up(pair, normed, gate_w, up_w):
    rows, depth = normed[0].shape
    width = gate_w[0].shape[1]
    total = rows * len(normed)
    half = depth // 2
    shape = (2, half, 2 * width) if width % 128 == 0 else (2, 2, half, width)
    return pl.pallas_call(
        gate_up_kernel,
        in_specs=[pl.BlockSpec(memory_space=pltpu.SMEM)]
        + [pl.BlockSpec(memory_space=pl.ANY)] * (len(normed) + 4),
        out_specs=pl.BlockSpec(memory_space=pltpu.VMEM),
        out_shape=jax.ShapeDtypeStruct((total, width), jnp.bfloat16),
        scratch_shapes=[
            pltpu.VMEM((len(normed), rows, depth), jnp.bfloat16),
            pltpu.VMEM(shape, jnp.bfloat16),
            pltpu.VMEM((len(normed), rows, width), jnp.float32),
            pltpu.VMEM((len(normed), rows, width), jnp.float32),
            pltpu.SemaphoreType.DMA((len(normed) + 4,)),
        ],
        compiler_params=pltpu.CompilerParams(vmem_limit_bytes=VMEM_LIMIT),
        cost_estimate=pl.CostEstimate(
            flops=4 * total * depth * width,
            bytes_accessed=2 * (total * depth + 2 * depth * width + total * width),
            transcendentals=total * width,
        ),
        name="gate_up",
    )(pair, *normed, gate_w[0], up_w[0], gate_w[1], up_w[1])


def down_kernel(*refs, n_parts):
    act_refs, w_refs, outs = refs[:n_parts], refs[n_parts : 2 * n_parts], refs[2 * n_parts : -3]
    acts, weight, sems = refs[-3:]
    width = act_refs[0].shape[1]
    rows = outs[0].shape[0]
    packed = len(acts.shape) == 2
    copies = []
    for i in range(n_parts):
        if packed:
            lanes = pl.ds(i * width, width)
            places = acts.at[:, lanes], weight.at[:, lanes]
        else:
            places = acts.at[i], weight.at[i]
        copies.append(pltpu.make_async_copy(act_refs[i], places[0], sems.at[2 * i]))
        copies.append(pltpu.make_async_copy(w_refs[i], places[1], sems.at[2 * i + 1]))
    for copy in copies:
        copy.start()
    for copy in copies:
        copy.wait()
    for k in range(len(outs) - 1, -1, -1):
        here = pl.ds(k * rows, rows)
        if packed:
            total = dot_rows(acts[here, :], weight[...])
        else:
            total = sum(dot_rows(acts[i, here, :], weight[i]) for i in range(n_parts))
        outs[k][...] = total.astype(outs[k].dtype)


def down(acts, weights):
    total, width = acts[0].shape
    columns = weights[0].shape[0]
    rows = total // GROUP
    n_parts = len(acts)
    if width % 128 == 0:
        shapes = [(total, n_parts * width), (columns, n_parts * width)]
    else:
        shapes = [(n_parts, total, width), (n_parts, columns, width)]
    return pl.pallas_call(
        functools.partial(down_kernel, n_parts=n_parts),
        out_shape=[
            jax.ShapeDtypeStruct((rows, columns), jnp.bfloat16 if i else jnp.float32)
            for i in range(GROUP)
        ],
        in_specs=[pl.BlockSpec(memory_space=pl.ANY)] * (2 * n_parts),
        out_specs=[pl.BlockSpec(memory_space=pltpu.VMEM)] * GROUP,
        scratch_shapes=[pltpu.VMEM(shape, jnp.bfloat16) for shape in shapes]
        + [pltpu.SemaphoreType.DMA((2 * n_parts,))],
        compiler_params=pltpu.CompilerParams(vmem_limit_bytes=VMEM_LIMIT),
        cost_estimate=pl.CostEstimate(
            flops=2 * total * width * columns * n_parts,
            bytes_accessed=2 * n_parts * (total + columns) * width + 2 * total * columns,
            transcendentals=0,
        ),
        name="down",
    )(*acts, *weights)


def finish_kernel(order, resid, own, *refs):
    total = resid[...].astype(jnp.float32) + own[...]
    for part in refs[:-1]:
        total = total + part[...].astype(jnp.float32)
    refs[-1][...] = total.astype(refs[-1].dtype)


def finish(order, out, own, parts):
    rows, columns = own.shape
    chunk = out.shape[1] // 4
    placed = pl.BlockSpec((rows, chunk), lambda d, order: (0, order[d]))
    plain = pl.BlockSpec((rows, chunk), lambda d, order: (0, d))
    return pl.pallas_call(
        finish_kernel,
        grid_spec=pltpu.PrefetchScalarGridSpec(
            num_scalar_prefetch=1,
            grid=(columns // chunk,),
            in_specs=[placed] + [plain] * (1 + len(parts)),
            out_specs=placed,
        ),
        out_shape=jax.ShapeDtypeStruct(out.shape, out.dtype),
        input_output_aliases={1: 0},
        compiler_params=pltpu.CompilerParams(vmem_limit_bytes=VMEM_LIMIT),
        cost_estimate=pl.CostEstimate(
            flops=rows * columns * 5, bytes_accessed=rows * columns * 14, transcendentals=0
        ),
        name="finish",
    )(order, out, own, *parts)


def swap(value, axis, size, bits):
    return lax.ppermute(value, axis, [(i, i ^ bits) for i in range(size)])


def per_device(
    q_in,
    kv_in,
    prefix_kv,
    hidden_in,
    q_gain,
    k_gain,
    post_gain,
    w_out,
    w_gate,
    w_up,
    w_down_t,
    lengths,
    row_group,
    owner_block,
):
    n_req, n_mlp = lax.axis_size("req"), lax.axis_size("mlp")
    me, core = lax.axis_index("req"), lax.axis_index("mlp")
    seat, place = me % GROUP, me // GROUP
    n_line = n_req // GROUP
    tok_count = q_in.shape[0]
    local_groups = kv_in.shape[2] // HD

    def exchange(block):
        width = block.shape[1] // GROUP
        parts = []
        for k in range(GROUP):
            part = lax.dynamic_slice_in_dim(block, (seat ^ k) * width, width, 1)
            parts.append(part if k == 0 else swap(part, "req", n_req, k))
        rows = jnp.take(jnp.stack(parts), jnp.arange(GROUP) ^ seat, axis=0)
        return rows.reshape(GROUP * block.shape[0], width)

    if n_line == 4:
        pair = place // 2
        inner = (place == 1) | (place == 2)

        def hop(value, *edges):
            return lax.ppermute(
                value, "req", [(GROUP * a + i, GROUP * b + i) for a, b in edges for i in range(GROUP)]
            )

        def near(rows):
            other = swap(rows, "req", n_req, GROUP)
            return jnp.where(
                place % 2 == 0,
                jnp.concatenate([rows, other], axis=0),
                jnp.concatenate([other, rows], axis=0),
            )

        def over(base):
            return hop(base, (1, 2), (2, 1))

        def far(crossed):
            return jnp.where(inner, crossed, hop(crossed, (1, 0), (2, 3)))

    else:
        pair = 0
        lines = [[line + GROUP * i for i in range(n_line)] for line in range(GROUP)]

        def near(rows):
            return lax.all_gather(rows, "req", axis_index_groups=lines, axis=0, tiled=True)

        def over(base):
            return base

        def far(crossed):
            return crossed

    def cores(part):
        return [part] + [swap(part, "mlp", n_mlp, k) for k in range(1, n_mlp)]

    held, slot, bit, weight = prefix_kv[None], jnp.argsort(owner_block) ^ me, n_req // 2, 1
    spot = 0
    while bit >= GROUP:
        held = jnp.concatenate([held, swap(held, "req", n_req, bit)], axis=0)
        spot = spot + (slot // bit) % 2 * weight
        bit, weight = bit // 2, weight * 2
    spot = spot + slot % GROUP * weight

    gate_rows = exchange(w_gate)
    up_rows = exchange(w_up)
    held, w_down_t = lax.optimization_barrier((held, w_down_t))
    held = jnp.stack([held] + [swap(held, "req", n_req, k) for k in range(1, GROUP)])
    held = held.reshape(n_req, 2, PB, local_groups * HD)
    picked = lax.dynamic_slice_in_dim(spot, row_group[0] * BPG, BPG, 0)
    chosen = jnp.take(held, picked, axis=0)
    down_rows = exchange(w_down_t)

    _, offset = slot_layout(lengths[0], tok_count)
    cosine, sine = rotation(offset + PLEN)
    start = (jnp.arange(tok_count, dtype=jnp.int32) - offset)[:, None]
    gains = q_gain[None], k_gain[None]
    first = local_groups // 2

    gate_base = near(gate_rows)
    chosen, gate_base = lax.optimization_barrier((chosen, gate_base))
    up_base = near(up_rows)
    gate_over = over(gate_base)
    attn_low = attention(start, cosine, sine, *gains, q_in, kv_in, chosen, 0, first)
    attn_low, gate_over, up_base, down_rows = lax.optimization_barrier(
        (attn_low, gate_over, up_base, down_rows)
    )
    down_base = near(down_rows)
    up_over = over(up_base)
    attn_high = attention(
        start, cosine, sine, *gains, q_in, kv_in, chosen, first, local_groups - first
    )

    sums = project(core[None], [attn_low, attn_high], w_out, n_mlp)
    parts = [swap(sums[k], "mlp", n_mlp, k) for k in range(1, n_mlp)]
    resid, own_normed = normalize(hidden_in, post_gain[None], sums[0], parts)
    normed = [own_normed] + [swap(own_normed, "req", n_req, k) for k in range(1, GROUP)]

    if n_line == 4:
        down_over = over(down_base)
        gate_w, up_w = (gate_base, far(gate_over)), (up_base, far(up_over))
        chunk = down_rows.shape[0]
        down_w = down_base, far(down_over[:chunk]), far(down_over[chunk:])
        order = [2 * pair, 2 * pair + 1, 2 - 2 * pair, 3 - 2 * pair]
    else:
        half = up_base.shape[0] // 2
        gate_w, up_w, down_w = (
            (base[:half], base[half:]) for base in (gate_base, up_base, down_base)
        )
        order = [0, 1, 2, 3]
    order = jnp.stack([jnp.asarray(entry, jnp.int32) for entry in order])
    pair = jnp.asarray(pair, jnp.int32)[None]

    gate_w, up_w, down_w = ([cores(part) for part in parts] for parts in (gate_w, up_w, down_w))
    acts = [
        gate_up(pair, normed, [part[k] for part in gate_w], [part[k] for part in up_w])
        for k in range(n_mlp)
    ]
    out, done = resid, 0
    for weights in down_w:
        sums = down(acts, weights)
        parts = [swap(sums[k], "req", n_req, k) for k in range(1, GROUP)]
        blocks = 4 * sums[0].shape[1] // resid.shape[1]
        out = finish(order[done : done + blocks], out, sums[0], parts)
        done += blocks
    return out


def solution(mesh):
    in_specs = (
        P("req", "mlp"),
        P(None, "req", "mlp"),
        P(None, "req", "mlp"),
        P(("req", "mlp"), None),
        P(),
        P(),
        P(),
        P("mlp", None),
        P("req", "mlp"),
        P("req", "mlp"),
        P("req", "mlp"),
        P("req", None),
        P("req"),
        P(),
    )
    out_specs = P(("req", "mlp"), None)
    return jax.shard_map(
        per_device, mesh=mesh, in_specs=in_specs, out_specs=out_specs, check_vma=False
    )
```

```python
import functools
import math

import jax
import jax.numpy as jnp
from jax import lax
from jax.experimental import pallas as pl
from jax.experimental.pallas import tpu as pltpu
from jax.sharding import PartitionSpec as P

HD = 128
PB = 64
PLEN = 512
BPG = 8
PARTNERS = (0, 1, 4, 5)
GROUP = len(PARTNERS)
VMEM_LIMIT = 48 * 1024 * 1024
SHORT = pl.CostEstimate(flops=1024, bytes_accessed=1024, transcendentals=0)


EPSILON = 1e-06
THETA = 1000000.0


def rotation(positions):
    half_width = HD // 2
    exponent = jnp.arange(half_width, dtype=jnp.float32) * (2.0 / HD)
    inv_freq = jnp.power(jnp.float32(THETA), -exponent)
    angles = positions.astype(jnp.float32)[:, None] * inv_freq[None, :]
    cosine, sine = jnp.cos(angles), jnp.sin(angles)
    return jnp.concatenate([cosine, cosine], axis=1), jnp.concatenate([-sine, sine], axis=1)


def slot_layout(row_lengths, tok_count):
    req_ends = jnp.cumsum(row_lengths)
    starts = req_ends - row_lengths
    slot_ids = jnp.arange(tok_count, dtype=jnp.int32)
    request = jnp.sum((slot_ids[:, None] >= req_ends[None, :]).astype(jnp.int32), axis=1)
    member = request[:, None] == jnp.arange(row_lengths.shape[0], dtype=jnp.int32)[None, :]
    offset = slot_ids - jnp.sum(jnp.where(member, starts[None, :], 0), axis=1)
    return (request, offset)


def dot_rows(left, right):
    return lax.dot_general(
        left, right, (((1,), (1,)), ((), ())), preferred_element_type=jnp.float32
    )


def attention_kernel(
    start_ref, cos_ref, sin_ref, q_gain, k_gain, q_ref, k_ref, v_ref, pk_ref, pv_ref, out_ref, bias
):
    tok_count = k_ref.shape[1]
    tile = min(256, tok_count)
    scale = math.log2(math.e) / math.sqrt(HD)

    @pl.when(pl.program_id(0) == 0)
    def _():
        keys = lax.broadcasted_iota(jnp.int32, (tok_count, tok_count), 1)
        slots = lax.broadcasted_iota(jnp.int32, (tok_count, tok_count), 0)
        seen = (keys >= start_ref[...]) & (keys <= slots)
        bias[...] = jnp.where(seen, 0.0, -1e30)

    def prepare(values, gain, rows):
        values = values.astype(jnp.float32)
        mean_sq = jnp.mean(values * values, axis=-1, keepdims=True)
        scaled = values * lax.rsqrt(mean_sq + EPSILON) * gain[...]
        turned = scaled * cos_ref[rows, :] + pltpu.roll(scaled, HD // 2, 1) * sin_ref[rows, :]
        return turned.astype(jnp.bfloat16)

    key = prepare(k_ref[0], k_gain, pl.ds(0, tok_count))
    value = v_ref[0]
    pre_key = pk_ref[...].reshape(-1, HD)
    pre_value = pv_ref[...].reshape(-1, HD)
    for head in range(q_ref.shape[1] // HD):
        lanes = pl.ds(head * HD, HD)
        for first in range(0, tok_count, tile):
            rows = pl.ds(first, tile)
            last = first + tile
            query = prepare(q_ref[rows, lanes], q_gain, rows)
            pre_w = jnp.exp2(dot_rows(query, pre_key) * scale)
            suf_w = jnp.exp2(dot_rows(query, key[:last]) * scale + bias[rows, :last])
            total = jnp.sum(pre_w, axis=-1, keepdims=True) + jnp.sum(suf_w, axis=-1, keepdims=True)
            top = jnp.dot(
                pre_w.astype(jnp.bfloat16), pre_value, preferred_element_type=jnp.float32
            ) + jnp.dot(
                suf_w.astype(jnp.bfloat16), value[:last], preferred_element_type=jnp.float32
            )
            out_ref[rows, lanes] = (top / total).astype(out_ref.dtype)


def attention(start, cosine, sine, q_gain, k_gain, q_in, kv_in, chosen, first, count):
    tok_count = q_in.shape[0]
    groups = kv_in.shape[2] // HD
    width = q_in.shape[1] // groups
    blocks = chosen.shape[0]

    def same(rows, columns):
        return pl.BlockSpec((rows, columns), lambda g: (0, 0))

    def suffix(which):
        return pl.BlockSpec((1, tok_count, HD), lambda g: (which, 0, g + first))

    def prefix(which):
        return pl.BlockSpec((blocks, 1, PB, HD), lambda g: (0, which, 0, g + first))

    keys = tok_count + PLEN
    return pl.pallas_call(
        attention_kernel,
        grid=(count,),
        in_specs=[
            same(tok_count, 1),
            same(tok_count, HD),
            same(tok_count, HD),
            same(1, HD),
            same(1, HD),
            pl.BlockSpec((tok_count, width), lambda g: (0, g + first)),
            suffix(0),
            suffix(1),
            prefix(0),
            prefix(1),
        ],
        out_specs=pl.BlockSpec((tok_count, width), lambda g: (0, g)),
        out_shape=jax.ShapeDtypeStruct((tok_count, count * width), jnp.bfloat16),
        scratch_shapes=[pltpu.VMEM((tok_count, tok_count), jnp.float32)],
        compiler_params=pltpu.CompilerParams(vmem_limit_bytes=VMEM_LIMIT),
        cost_estimate=SHORT,
        name="attention",
    )(start, cosine, sine, q_gain, k_gain, q_in, kv_in, kv_in, chosen, chosen)


def project_kernel(core, *refs, n_parts, n_mlp):
    parts, weights, outs = refs[:n_parts], refs[n_parts : 2 * n_parts], refs[2 * n_parts :]
    rows = outs[0].shape[0]
    for k in range(n_mlp - 1, -1, -1):
        part = pl.ds(pl.multiple_of((core[0] ^ k) * rows, rows), rows)
        total = 0.0
        for x, w in zip(parts, weights):
            total = total + jnp.dot(x[part, :], w[...], preferred_element_type=jnp.float32)
        outs[k][...] = total.astype(outs[k].dtype)


def project(core, parts, w_out, n_mlp):
    tok_count, depth = parts[0].shape
    columns = w_out.shape[1]
    rows, tile = tok_count // n_mlp, 512
    n_parts = len(parts)
    return pl.pallas_call(
        functools.partial(project_kernel, n_parts=n_parts, n_mlp=n_mlp),
        grid_spec=pltpu.PrefetchScalarGridSpec(
            num_scalar_prefetch=1,
            grid=(columns // tile,),
            in_specs=[pl.BlockSpec((tok_count, depth), lambda n, core: (0, 0))] * n_parts
            + [
                pl.BlockSpec((depth, tile), functools.partial(lambda i, n, core: (i, n), i))
                for i in range(n_parts)
            ],
            out_specs=[pl.BlockSpec((rows, tile), lambda n, core: (0, n))] * n_mlp,
        ),
        out_shape=[
            jax.ShapeDtypeStruct((rows, columns), jnp.bfloat16 if k else jnp.float32)
            for k in range(n_mlp)
        ],
        compiler_params=pltpu.CompilerParams(vmem_limit_bytes=VMEM_LIMIT),
        cost_estimate=SHORT,
        name="project",
    )(core, *parts, *[w_out] * n_parts)


def normalize_kernel(hidden, gain, own, *refs):
    parts, resid_ref, normed_ref = refs[:-2], refs[-2], refs[-1]
    total = hidden[...].astype(jnp.float32) + own[...]
    for part in parts:
        total = total + part[...].astype(jnp.float32)
    resid = total.astype(resid_ref.dtype)
    resid_ref[...] = resid
    values = resid.astype(jnp.float32)
    mean_sq = jnp.mean(values * values, axis=-1, keepdims=True)
    normed = values * lax.rsqrt(mean_sq + EPSILON) * gain[...]
    normed_ref[...] = normed.astype(normed_ref.dtype)


def normalize(hidden, gain, own, parts):
    rows, columns = hidden.shape
    tile = min(64, rows)
    spec = pl.BlockSpec((tile, columns), lambda i: (i, 0))
    return pl.pallas_call(
        normalize_kernel,
        grid=(rows // tile,),
        in_specs=[spec, pl.BlockSpec((1, columns), lambda i: (0, 0)), spec] + [spec] * len(parts),
        out_specs=[spec, spec],
        out_shape=[jax.ShapeDtypeStruct(hidden.shape, hidden.dtype)] * 2,
        compiler_params=pltpu.CompilerParams(vmem_limit_bytes=VMEM_LIMIT),
        cost_estimate=SHORT,
        name="normalize",
    )(hidden, gain, own, *parts)


def move_kernel(scalar, *refs, n_in, plan):
    sems = refs[-1]
    copies = [
        pltpu.make_async_copy(src, dst, sems.at[i])
        for i, (src, dst) in enumerate(plan(scalar[0], refs[:n_in], refs[n_in:-1]))
    ]
    for copy in copies:
        copy.start()
    for copy in copies:
        copy.wait()


def move(scalar, arrays, shapes, plan, n_copies, name):
    anywhere = pl.BlockSpec(memory_space=pl.ANY)
    return pl.pallas_call(
        functools.partial(move_kernel, n_in=len(arrays), plan=plan),
        in_specs=[pl.BlockSpec(memory_space=pltpu.SMEM)] + [anywhere] * len(arrays),
        out_specs=[pl.BlockSpec(memory_space=pltpu.VMEM)] * len(shapes),
        out_shape=[jax.ShapeDtypeStruct(shape, jnp.bfloat16) for shape in shapes],
        scratch_shapes=[pltpu.SemaphoreType.DMA((n_copies,))],
        compiler_params=pltpu.CompilerParams(vmem_limit_bytes=VMEM_LIMIT),
        cost_estimate=SHORT,
        name=name,
    )(scalar, *arrays)


def cut(seat, blocks):
    rows, columns = blocks[0].shape
    width = columns // GROUP
    if width % 128:
        return [
            jnp.stack(
                [lax.dynamic_slice_in_dim(x, (seat[0] ^ j) * width, width, 1) for x in blocks]
            )
            for j in range(GROUP)
        ]

    def plan(seat, sources, targets):
        return [
            (source.at[:, pl.ds(pl.multiple_of((seat ^ j) * width, 128), width)], targets[j].at[m])
            for j in range(GROUP)
            for m, source in enumerate(sources)
        ]

    shapes = [(len(blocks), rows, width)] * GROUP
    return move(seat, blocks, shapes, plan, GROUP * len(blocks), "cut")


def merge(seat, parts, groups):
    _, rows, width = parts[0].shape
    if width % 128:
        whole = jnp.stack(parts, axis=1)
        return [jnp.stack([whole[m] for m in group]) for group in groups]

    def plan(_, sources, targets):
        return [
            (source.at[m], target.at[i, j])
            for target, group in zip(targets, groups)
            for i, m in enumerate(group)
            for j, source in enumerate(sources)
        ]

    shapes = [(len(group), GROUP, rows, width) for group in groups]
    return move(seat, parts, shapes, plan, GROUP * sum(map(len, groups)), "merge")


def collect(seat, entries):
    shape = entries[0][0].shape[1:]
    if shape[-1] % 128:
        return jnp.stack([array[m] for array, m in entries])

    def plan(_, sources, targets):
        return [
            (source.at[m], targets[0].at[i])
            for i, (source, (_, m)) in enumerate(zip(sources, entries))
        ]

    arrays = [array for array, _ in entries]
    return move(seat, arrays, [(len(entries), *shape)], plan, len(entries), "collect")[0]


def weight_copies(me, refs, keys, target, mask, sems):
    copies = []
    for i, ref in enumerate(refs):
        part, entry = divmod(i, len(keys))
        rows, width = ref.shape[-2:]
        packed = len(target.shape) == 2
        lanes = pl.ds(part * width, width)
        if keys[entry] is None:
            place = target.at[:, lanes] if packed else target.at[part]
            copies.append(pltpu.make_async_copy(ref.at[0], place, sems.at[len(copies)]))
            continue
        for k, key in enumerate(keys[entry]):
            for j, partner in enumerate(PARTNERS):
                source = (me ^ (key ^ partner)) & mask
                here = pl.ds(pl.multiple_of(source * rows, 8), rows)
                place = target.at[here, lanes] if packed else target.at[part, here]
                copies.append(pltpu.make_async_copy(ref.at[k, j], place, sems.at[len(copies)]))
    return copies


def expand_kernel(me, *refs, n_parts, keys, second):
    n_weights = n_parts * len(keys)
    x_refs, refs = refs[: GROUP + 1], refs[GROUP + 1 :]
    w_refs, refs = refs[:n_weights], refs[n_weights:]
    before, refs = (refs[:n_parts], refs[n_parts:]) if second else ((), refs)
    outs, (x_all, weight, x_sems, w_sems) = refs[:n_parts], refs[n_parts:]
    width = outs[0].shape[1]
    rows, depth = x_refs[0].shape
    packed = len(weight.shape) == 2
    places = [x_all.at[i] for i in range(GROUP - 1)]
    places += [x_all.at[GROUP - 1, pl.ds(i * rows // 2, rows // 2)] for i in range(2)]
    copies = weight_copies(me[0], w_refs, keys, weight, -1, w_sems)
    copies += [
        pltpu.make_async_copy(x_ref, place, x_sems.at[i])
        for i, (x_ref, place) in enumerate(zip(x_refs, places))
    ]
    for copy in copies:
        copy.start()
    for copy in copies:
        copy.wait()

    def step(i, carry):
        x = x_all[i]
        lines = pl.ds(pl.multiple_of(i * rows, rows), rows)
        if packed:
            whole = jnp.dot(x, weight[...], preferred_element_type=jnp.float32)
        for part in range(n_parts):
            if packed:
                total = whole[:, part * width : (part + 1) * width]
            else:
                total = jnp.dot(x, weight[part], preferred_element_type=jnp.float32)
            if second:
                total = total * before[part][lines, :]
            else:
                total = total / (1.0 + jnp.exp(-total))
            outs[part][lines, :] = total.astype(outs[part].dtype)
        return carry

    lax.fori_loop(0, GROUP, step, 0)


def expand(me, normed, keys, weights, before=()):
    rows, depth = normed[0].shape
    n_parts = len(weights)
    width = weights[0][0].shape[-1]
    total = rows * GROUP
    n_copies = n_parts * GROUP * sum(len(entry or (0,)) for entry in keys)
    shape = (depth, n_parts * width) if width % 128 == 0 else (n_parts, depth, width)
    kind = jnp.bfloat16 if before else jnp.float32
    vmem, anywhere = pl.BlockSpec(memory_space=pltpu.VMEM), pl.BlockSpec(memory_space=pl.ANY)
    return pl.pallas_call(
        functools.partial(
            expand_kernel, n_parts=n_parts, keys=keys, second=bool(before)
        ),
        in_specs=[pl.BlockSpec(memory_space=pltpu.SMEM)]
        + [anywhere] * (len(normed) + n_parts * len(keys))
        + [vmem] * len(before),
        out_specs=[vmem] * n_parts,
        out_shape=[jax.ShapeDtypeStruct((total, width), kind)] * n_parts,
        scratch_shapes=[
            pltpu.VMEM((GROUP, rows, depth), jnp.bfloat16),
            pltpu.VMEM(shape, jnp.bfloat16),
            pltpu.SemaphoreType.DMA((len(normed),)),
            pltpu.SemaphoreType.DMA((n_copies,)),
        ],
        compiler_params=pltpu.CompilerParams(vmem_limit_bytes=VMEM_LIMIT),
        cost_estimate=SHORT,
        name="up" if before else "gate",
    )(me, *normed, *[array for part in weights for array in part], *before)


def down_kernel(me, *refs, n_parts, keys, mask):
    n_weights = n_parts * len(keys)
    act_refs, w_refs = refs[:n_parts], refs[n_parts : n_parts + n_weights]
    own, to_x, to_y, keep_x, keep_y, acts, weight, a_sems, w_sems = refs[n_parts + n_weights :]
    width = act_refs[0].shape[1]
    rows = own.shape[0]
    half = rows // 2
    packed = len(acts.shape) == 2
    copies = weight_copies(me[0], w_refs, keys, weight, mask, w_sems)
    for i in range(n_parts):
        place = acts.at[:, pl.ds(i * width, width)] if packed else acts.at[i]
        copies.append(pltpu.make_async_copy(act_refs[i], place, a_sems.at[i]))
    for copy in copies:
        copy.start()
    for copy in copies:
        copy.wait()

    def sums(block):
        here = pl.ds(block * rows, rows)
        if packed:
            return dot_rows(acts[here, :], weight[...])
        return sum(dot_rows(acts[i, here, :], weight[i]) for i in range(n_parts))

    total = sums(3).astype(jnp.bfloat16)
    to_x[half:, :] = total[:half]
    to_y[half:, :] = total[half:]
    total = sums(1)
    to_x[:half, :] = total[:half].astype(jnp.bfloat16)
    keep_x[...] = total[half:]
    total = sums(2)
    to_y[:half, :] = total[half:].astype(jnp.bfloat16)
    keep_y[...] = total[:half]
    own[...] = sums(0)


def down(me, acts, keys, weights, mask):
    total, width = acts[0].shape
    n_parts = len(acts)
    columns = sum(math.prod(array.shape[:-1]) for array in weights[0])
    rows = total // GROUP
    if width % 128 == 0:
        shapes = [(total, n_parts * width), (columns, n_parts * width)]
    else:
        shapes = [(n_parts, total, width), (n_parts, columns, width)]
    outs = [(rows, jnp.float32), (rows, jnp.bfloat16), (rows, jnp.bfloat16)]
    outs += [(rows // 2, jnp.float32)] * 2
    return pl.pallas_call(
        functools.partial(down_kernel, n_parts=n_parts, keys=keys, mask=mask),
        out_shape=[jax.ShapeDtypeStruct((length, columns), dtype) for length, dtype in outs],
        in_specs=[pl.BlockSpec(memory_space=pltpu.SMEM)]
        + [pl.BlockSpec(memory_space=pl.ANY)] * (n_parts + n_parts * len(keys)),
        out_specs=[pl.BlockSpec(memory_space=pltpu.VMEM)] * 5,
        scratch_shapes=[pltpu.VMEM(shape, jnp.bfloat16) for shape in shapes]
        + [
            pltpu.SemaphoreType.DMA((n_parts,)),
            pltpu.SemaphoreType.DMA((n_parts * GROUP * sum(len(entry or (0,)) for entry in keys),)),
        ],
        compiler_params=pltpu.CompilerParams(vmem_limit_bytes=VMEM_LIMIT),
        cost_estimate=SHORT,
        name="down",
    )(me, *acts, *[array for part in weights for array in part])


def finish_kernel(upper, resid, *refs):
    out_ref = refs[-1]
    half, width = resid.shape[0] // 2, resid.shape[1] // 2
    for piece in range(2):
        own, from_x, from_y, late_x, late_y = refs[5 * piece : 5 * piece + 5]
        here = pl.ds(pl.multiple_of((upper[0] ^ piece) * width, 128), width)
        for rows, first, late in (
            (pl.ds(0, half), from_x, late_y),
            (pl.ds(half, half), from_y, late_x),
        ):
            total = resid[rows, here].astype(jnp.float32) + own[rows, :]
            total = total + first[:half, :].astype(jnp.float32) + late[...].astype(jnp.float32)
            out_ref[rows, here] = total.astype(out_ref.dtype)


def finish(upper, resid, pieces):
    vmem = pl.BlockSpec(memory_space=pltpu.VMEM)
    return pl.pallas_call(
        finish_kernel,
        in_specs=[pl.BlockSpec(memory_space=pltpu.SMEM)] + [vmem] * 11,
        out_specs=vmem,
        out_shape=jax.ShapeDtypeStruct(resid.shape, resid.dtype),
        compiler_params=pltpu.CompilerParams(vmem_limit_bytes=VMEM_LIMIT),
        cost_estimate=SHORT,
        name="finish",
    )(upper, resid, *[part for piece in pieces for part in piece])


def swap(value, axis, size, bits):
    return lax.ppermute(value, axis, [(i, i ^ bits) for i in range(size)])


def per_device(
    q_in,
    kv_in,
    prefix_kv,
    hidden_in,
    q_gain,
    k_gain,
    post_gain,
    w_out,
    w_gate,
    w_up,
    w_down_t,
    lengths,
    row_group,
    owner_block,
):
    n_req, n_mlp = lax.axis_size("req"), lax.axis_size("mlp")
    me, core = lax.axis_index("req"), lax.axis_index("mlp")
    tok_count = q_in.shape[0]
    local_groups = kv_in.shape[2] // HD

    def tie(tree):
        leaves, shape = jax.tree.flatten(tree)
        fixed = [isinstance(leaf, int) for leaf in leaves]
        held = iter(lax.optimization_barrier([x for x, f in zip(leaves, fixed) if not f]))
        return jax.tree.unflatten(shape, [x if f else next(held) for x, f in zip(leaves, fixed)])

    top = n_req // 2
    others = [1 << i for i in range(n_req.bit_length()) if 1 << i < n_req and 1 << i not in PARTNERS]
    others = others[::-1]
    seat = ((me & 1) + (me >> 2 & 1) * 2)[None]
    place, upper = me[None], (me // top)[None]

    def req(value, key):
        return swap(value, "req", n_req, key)

    def cores(part):
        return [part] + [swap(part, "mlp", n_mlp, k) for k in range(1, n_mlp)]

    def trade(parts):
        return [parts[0]] + [req(part, key) for part, key in zip(parts[1:], PARTNERS[1:])]

    def relay(entry, key):
        array, m = entry
        return (req(array if array.shape[0] == 1 else array[m : m + 1], key), 0)

    def complete(entries):
        for key in others[1:]:
            for held_key in list(entries):
                if held_key ^ key not in entries:
                    entries[held_key ^ key] = relay(entries[held_key], key)
        return entries

    def share(entries, *keys):
        return [(keys, cores(collect(seat, [entries[key] for key in keys])))]

    def gather(shares, count):
        keys, parts = [keys for keys, _ in shares], list(zip(*[parts for _, parts in shares]))
        if parts[0][0].shape[2] % 16 == 0:
            return keys, [list(part) for part in parts]
        spots = [(key ^ partner) % count for entry in keys for key in entry for partner in PARTNERS]
        spots = jnp.asarray([spots.index(i) for i in range(count)])
        spots = spots[(me ^ jnp.arange(count)) % count]
        ordered = []
        for part in parts:
            whole = jnp.concatenate(part, axis=0)
            whole = whole.reshape(count, *whole.shape[2:])
            ordered.append([jnp.take(whole, spots, axis=0).reshape(1, -1, whole.shape[-1])])
        return [None], ordered

    planes = [prefix_kv] + [req(prefix_kv, 4 * k) for k in range(1, n_req // 4)]
    held = jnp.stack(planes)
    slot = jnp.argsort(owner_block) ^ me
    spot = slot // 4 + slot % 4 * (n_req // 4)
    picked = lax.dynamic_slice_in_dim(spot, row_group[0] * BPG, BPG, 0)

    parts = list(cut(seat, [w_gate, w_up]))
    held, parts[3] = tie((held, parts[3]))
    open_w, gate_own, up_own = merge(seat, trade(parts), [(0, 1), (0,), (1,)])
    last = others[-1]
    held = jnp.stack([held] + [req(held, k) for k in range(1, 4)])
    held = held.reshape(n_req, 2, PB, local_groups * HD)
    chosen = jnp.take(held, picked, axis=0)
    gate_top, open_last = req(gate_own, top), req(open_w, last)

    _, offset = slot_layout(lengths[0], tok_count)
    cosine, sine = rotation(offset + PLEN)
    start = (jnp.arange(tok_count, dtype=jnp.int32) - offset)[:, None]
    gains = q_gain[None], k_gain[None]

    chosen, cosine, sine, start = tie((chosen, cosine, sine, start))
    attn = attention(start, cosine, sine, *gains, q_in, kv_in, chosen, 0, local_groups)
    attn, gate_top, up_own, w_down_t = tie((attn, gate_top, up_own, w_down_t))
    down_parts = trade(cut(seat, [w_down_t]))

    own_rows = hidden_in.shape[0]
    sums = project(core[None], [attn], w_out, n_mlp)
    parts = [swap(sums[k], "mlp", n_mlp, k) for k in range(1, n_mlp)]
    resid, own_normed = normalize(hidden_in, post_gain[None], sums[0], parts)

    own_normed, open_last, down_parts, up_own = tie((own_normed, open_last, down_parts, up_own))
    gate_w = {0: (gate_own, 0), last: (open_last, 0), top: (gate_top, 0)}

    half = own_rows // 2
    key_x, key_y = PARTNERS[1:3]
    next_x, next_y = req(own_normed, key_x), req(own_normed, key_y)
    up_top = req(up_own, top)
    (down_own,) = merge(seat, down_parts, [(0,)])
    gate_all = share(gate_w, *gate_w)
    gate_rest = {key: v for key, v in complete(dict(gate_w)).items() if key not in gate_w}
    next_x, next_y, up_top, down_own, gate_all, gate_rest = tie(
        (next_x, next_y, up_top, down_own, gate_all, gate_rest)
    )
    diag = [req(next_x[:half], key_y), req(next_y[half:], key_x)]
    up_w = {0: (up_own, 0), last: (open_last, 1), top: (up_top, 0)}
    up_all = share(up_w, *up_w)
    up_rest = {key: v for key, v in complete(dict(up_w)).items() if key not in up_w}
    gate_all = gate_all + [([key], cores(v[0])) for key, v in gate_rest.items()]
    diag, up_all, up_rest, gate_all, down_own = tie((diag, up_all, up_rest, gate_all, down_own))
    normed = [own_normed, next_x, next_y] + diag

    opened = expand(place, normed, *gather(gate_all, n_req))
    up_all = up_all + [([key], cores(v[0])) for key, v in up_rest.items()]
    down_top, down_last = req(down_own, top), req(down_own, last)
    near = [([0], cores(down_own))]
    opened, up_all, near = tie((opened, up_all, near))
    acts = expand(place, normed, *gather(up_all, n_req), opened)
    acts, down_top, down_last = tie((acts, down_top, down_last))
    down_w = complete({0: (down_own, 0), last: (down_last, 0), top: (down_top, 0)})
    near = near + [([key], cores(v[0])) for key, v in down_w.items() if key and not key & top]
    far = [([key], v[0]) for key, v in down_w.items() if key & top]

    sums, parts = [], down(place, acts, *gather(near, top), top - 1)
    for piece in range(2):
        own, to_x, to_y, keep_x, keep_y = parts
        from_x, from_y = req(to_x, key_x), req(to_y, key_y)
        if piece == 0:
            far, from_x, from_y = tie((far, from_x, from_y))
            far = [(keys, cores(array)) for keys, array in far]
            parts = down(place, acts, *gather(far, top), top - 1)
        late_y = keep_y + from_x[half:].astype(jnp.float32)
        late_x = keep_x + from_y[half:].astype(jnp.float32)
        late_y = req(late_y.astype(jnp.bfloat16), key_y)
        late_x = req(late_x.astype(jnp.bfloat16), key_x)
        sums.append([own, from_x, from_y, late_x, late_y])
    return finish(upper, resid, sums)


def solution(mesh):
    in_specs = (
        P("req", "mlp"),
        P(None, "req", "mlp"),
        P(None, "req", "mlp"),
        P(("req", "mlp"), None),
        P(),
        P(),
        P(),
        P("mlp", None),
        P("req", "mlp"),
        P("req", "mlp"),
        P("req", "mlp"),
        P("req", None),
        P("req"),
        P(),
    )
    out_specs = P(("req", "mlp"), None)
    return jax.shard_map(
        per_device, mesh=mesh, in_specs=in_specs, out_specs=out_specs, check_vma=False
    )
```

```python
import functools
import math

import jax
import jax.numpy as jnp
from jax import lax
from jax.experimental import pallas as pl
from jax.experimental.pallas import tpu as pltpu
from jax.sharding import PartitionSpec as P

HD = 128
PB = 64
PLEN = 512
BPG = 8
PARTNERS = (0, 1, 4, 5)
GROUP = len(PARTNERS)
VMEM_LIMIT = 48 * 1024 * 1024
SHORT = pl.CostEstimate(flops=1024, bytes_accessed=1024, transcendentals=0)


EPSILON = 1e-06
THETA = 1000000.0


def rotation(positions):
    half_width = HD // 2
    exponent = jnp.arange(half_width, dtype=jnp.float32) * (2.0 / HD)
    inv_freq = jnp.power(jnp.float32(THETA), -exponent)
    angles = positions.astype(jnp.float32)[:, None] * inv_freq[None, :]
    cosine, sine = jnp.cos(angles), jnp.sin(angles)
    return jnp.concatenate([cosine, cosine], axis=1), jnp.concatenate([-sine, sine], axis=1)


def slot_layout(row_lengths, tok_count):
    req_ends = jnp.cumsum(row_lengths)
    starts = req_ends - row_lengths
    slot_ids = jnp.arange(tok_count, dtype=jnp.int32)
    request = jnp.sum((slot_ids[:, None] >= req_ends[None, :]).astype(jnp.int32), axis=1)
    member = request[:, None] == jnp.arange(row_lengths.shape[0], dtype=jnp.int32)[None, :]
    offset = slot_ids - jnp.sum(jnp.where(member, starts[None, :], 0), axis=1)
    return (request, offset)


def dot_rows(left, right):
    return lax.dot_general(
        left, right, (((1,), (1,)), ((), ())), preferred_element_type=jnp.float32
    )


def attention_kernel(
    start_ref, cos_ref, sin_ref, q_gain, k_gain, q_ref, k_ref, v_ref, pk_ref, pv_ref, out_ref, bias
):
    tok_count = k_ref.shape[1]
    tile = min(256, tok_count)
    scale = math.log2(math.e) / math.sqrt(HD)

    @pl.when(pl.program_id(0) == 0)
    def _():
        keys = lax.broadcasted_iota(jnp.int32, (tok_count, tok_count), 1)
        slots = lax.broadcasted_iota(jnp.int32, (tok_count, tok_count), 0)
        seen = (keys >= start_ref[...]) & (keys <= slots)
        bias[...] = jnp.where(seen, 0.0, -1e30)

    def prepare(values, gain, rows):
        values = values.astype(jnp.float32)
        mean_sq = jnp.mean(values * values, axis=-1, keepdims=True)
        scaled = values * lax.rsqrt(mean_sq + EPSILON) * gain[...]
        turned = scaled * cos_ref[rows, :] + pltpu.roll(scaled, HD // 2, 1) * sin_ref[rows, :]
        return turned.astype(jnp.bfloat16)

    key = prepare(k_ref[0], k_gain, pl.ds(0, tok_count))
    value = v_ref[0]
    pre_key = pk_ref[...].reshape(-1, HD)
    pre_value = pv_ref[...].reshape(-1, HD)
    for head in range(q_ref.shape[1] // HD):
        lanes = pl.ds(head * HD, HD)
        for first in range(0, tok_count, tile):
            rows = pl.ds(first, tile)
            last = first + tile
            query = prepare(q_ref[rows, lanes], q_gain, rows)
            pre_w = jnp.exp2(dot_rows(query, pre_key) * scale)
            suf_w = jnp.exp2(dot_rows(query, key[:last]) * scale + bias[rows, :last])
            total = jnp.sum(pre_w, axis=-1, keepdims=True) + jnp.sum(suf_w, axis=-1, keepdims=True)
            top = jnp.dot(
                pre_w.astype(jnp.bfloat16), pre_value, preferred_element_type=jnp.float32
            ) + jnp.dot(
                suf_w.astype(jnp.bfloat16), value[:last], preferred_element_type=jnp.float32
            )
            out_ref[rows, lanes] = (top / total).astype(out_ref.dtype)


def attention(start, cosine, sine, q_gain, k_gain, q_in, kv_in, chosen, first, count):
    tok_count = q_in.shape[0]
    groups = kv_in.shape[2] // HD
    width = q_in.shape[1] // groups
    blocks = chosen.shape[0]

    def same(rows, columns):
        return pl.BlockSpec((rows, columns), lambda g: (0, 0))

    def suffix(which):
        return pl.BlockSpec((1, tok_count, HD), lambda g: (which, 0, g + first))

    def prefix(which):
        return pl.BlockSpec((blocks, 1, PB, HD), lambda g: (0, which, 0, g + first))

    keys = tok_count + PLEN
    return pl.pallas_call(
        attention_kernel,
        grid=(count,),
        in_specs=[
            same(tok_count, 1),
            same(tok_count, HD),
            same(tok_count, HD),
            same(1, HD),
            same(1, HD),
            pl.BlockSpec((tok_count, width), lambda g: (0, g + first)),
            suffix(0),
            suffix(1),
            prefix(0),
            prefix(1),
        ],
        out_specs=pl.BlockSpec((tok_count, width), lambda g: (0, g)),
        out_shape=jax.ShapeDtypeStruct((tok_count, count * width), jnp.bfloat16),
        scratch_shapes=[pltpu.VMEM((tok_count, tok_count), jnp.float32)],
        compiler_params=pltpu.CompilerParams(vmem_limit_bytes=VMEM_LIMIT),
        cost_estimate=SHORT,
        name="attention",
    )(start, cosine, sine, q_gain, k_gain, q_in, kv_in, kv_in, chosen, chosen)


def project_kernel(core, *refs, n_parts, n_mlp):
    parts, weights, outs = refs[:n_parts], refs[n_parts : 2 * n_parts], refs[2 * n_parts :]
    rows = outs[0].shape[0]
    for k in range(n_mlp - 1, -1, -1):
        part = pl.ds(pl.multiple_of((core[0] ^ k) * rows, rows), rows)
        total = 0.0
        for x, w in zip(parts, weights):
            total = total + jnp.dot(x[part, :], w[...], preferred_element_type=jnp.float32)
        outs[k][...] = total.astype(outs[k].dtype)


def project(core, parts, w_out, n_mlp):
    tok_count, depth = parts[0].shape
    columns = w_out.shape[1]
    rows, tile = tok_count // n_mlp, 512
    n_parts = len(parts)
    return pl.pallas_call(
        functools.partial(project_kernel, n_parts=n_parts, n_mlp=n_mlp),
        grid_spec=pltpu.PrefetchScalarGridSpec(
            num_scalar_prefetch=1,
            grid=(columns // tile,),
            in_specs=[pl.BlockSpec((tok_count, depth), lambda n, core: (0, 0))] * n_parts
            + [
                pl.BlockSpec((depth, tile), functools.partial(lambda i, n, core: (i, n), i))
                for i in range(n_parts)
            ],
            out_specs=[pl.BlockSpec((rows, tile), lambda n, core: (0, n))] * n_mlp,
        ),
        out_shape=[
            jax.ShapeDtypeStruct((rows, columns), jnp.bfloat16 if k else jnp.float32)
            for k in range(n_mlp)
        ],
        compiler_params=pltpu.CompilerParams(vmem_limit_bytes=VMEM_LIMIT),
        cost_estimate=SHORT,
        name="project",
    )(core, *parts, *[w_out] * n_parts)


def normalize_kernel(hidden, gain, own, *refs):
    parts, resid_ref, normed_ref = refs[:-2], refs[-2], refs[-1]
    total = hidden[...].astype(jnp.float32) + own[...]
    for part in parts:
        total = total + part[...].astype(jnp.float32)
    resid = total.astype(resid_ref.dtype)
    resid_ref[...] = resid
    values = resid.astype(jnp.float32)
    mean_sq = jnp.mean(values * values, axis=-1, keepdims=True)
    normed = values * lax.rsqrt(mean_sq + EPSILON) * gain[...]
    normed_ref[...] = normed.astype(normed_ref.dtype)


def normalize(hidden, gain, own, parts):
    rows, columns = hidden.shape
    tile = min(64, rows)
    spec = pl.BlockSpec((tile, columns), lambda i: (i, 0))
    return pl.pallas_call(
        normalize_kernel,
        grid=(rows // tile,),
        in_specs=[spec, pl.BlockSpec((1, columns), lambda i: (0, 0)), spec] + [spec] * len(parts),
        out_specs=[spec, spec],
        out_shape=[jax.ShapeDtypeStruct(hidden.shape, hidden.dtype)] * 2,
        compiler_params=pltpu.CompilerParams(vmem_limit_bytes=VMEM_LIMIT),
        cost_estimate=SHORT,
        name="normalize",
    )(hidden, gain, own, *parts)


def move_kernel(scalar, *refs, n_in, plan):
    sems = refs[-1]
    copies = [
        pltpu.make_async_copy(src, dst, sems.at[i])
        for i, (src, dst) in enumerate(plan(scalar[0], refs[:n_in], refs[n_in:-1]))
    ]
    for copy in copies:
        copy.start()
    for copy in copies:
        copy.wait()


def move(scalar, arrays, shapes, plan, n_copies, name):
    anywhere = pl.BlockSpec(memory_space=pl.ANY)
    return pl.pallas_call(
        functools.partial(move_kernel, n_in=len(arrays), plan=plan),
        in_specs=[pl.BlockSpec(memory_space=pltpu.SMEM)] + [anywhere] * len(arrays),
        out_specs=[pl.BlockSpec(memory_space=pltpu.VMEM)] * len(shapes),
        out_shape=[jax.ShapeDtypeStruct(shape, jnp.bfloat16) for shape in shapes],
        scratch_shapes=[pltpu.SemaphoreType.DMA((n_copies,))],
        compiler_params=pltpu.CompilerParams(vmem_limit_bytes=VMEM_LIMIT),
        cost_estimate=SHORT,
        name=name,
    )(scalar, *arrays)


def cut(seat, blocks):
    rows, columns = blocks[0].shape
    width = columns // GROUP
    if width % 128:
        return [
            jnp.stack(
                [lax.dynamic_slice_in_dim(x, (seat[0] ^ j) * width, width, 1) for x in blocks]
            )
            for j in range(GROUP)
        ]

    def plan(seat, sources, targets):
        return [
            (source.at[:, pl.ds(pl.multiple_of((seat ^ j) * width, 128), width)], targets[j].at[m])
            for j in range(GROUP)
            for m, source in enumerate(sources)
        ]

    shapes = [(len(blocks), rows, width)] * GROUP
    return move(seat, blocks, shapes, plan, GROUP * len(blocks), "cut")


def merge(seat, parts):
    n_mats, rows, width = parts[0].shape
    if width % 128:
        return jnp.stack(parts, axis=1)

    def plan(_, sources, targets):
        return [
            (source.at[m], targets[0].at[m, j])
            for j, source in enumerate(sources)
            for m in range(n_mats)
        ]

    shapes = [(n_mats, GROUP, rows, width)]
    return move(seat, parts, shapes, plan, GROUP * n_mats, "merge")[0]


def weight_copies(me, refs, keys, matrix, target, mask, sems):
    copies = []
    for i, ref in enumerate(refs):
        part, entry = divmod(i, len(keys))
        rows, width = ref.shape[-2:]
        packed = len(target.shape) == 2
        lanes = pl.ds(part * width, width)
        if keys[entry] is None:
            place = target.at[:, lanes] if packed else target.at[part]
            copies.append(pltpu.make_async_copy(ref.at[matrix], place, sems.at[len(copies)]))
            continue
        for k, key in enumerate(keys[entry]):
            for j, partner in enumerate(PARTNERS):
                source = (me ^ (key ^ partner)) & mask
                here = pl.ds(pl.multiple_of(source * rows, 8), rows)
                place = target.at[here, lanes] if packed else target.at[part, here]
                copies.append(pltpu.make_async_copy(ref.at[matrix * len(keys[entry]) + k, j], place, sems.at[len(copies)]))
    return copies


def expand_kernel(me, *refs, n_parts, keys):
    n_weights = n_parts * len(keys)
    x_refs, refs = refs[: GROUP + 1], refs[GROUP + 1 :]
    w_refs, outs, refs = refs[:n_weights], refs[n_weights : n_weights + n_parts], refs[n_weights + n_parts :]
    x_all, gate_w, up_w, opened, x_sems, gate_sems, up_sems = refs
    width = outs[0].shape[1]
    rows, depth = x_refs[0].shape
    places = [x_all.at[i] for i in range(GROUP - 1)]
    places += [x_all.at[GROUP - 1, pl.ds(i * rows // 2, rows // 2)] for i in range(2)]
    first = weight_copies(me[0], w_refs, keys, 0, gate_w, -1, gate_sems)
    first += [
        pltpu.make_async_copy(x_ref, place, x_sems.at[i])
        for i, (x_ref, place) in enumerate(zip(x_refs, places))
    ]
    second = weight_copies(me[0], w_refs, keys, 1, up_w, -1, up_sems)
    for copy in first + second:
        copy.start()

    def product(x, weight):
        if len(weight.shape) == 2:
            whole = jnp.dot(x, weight[...], preferred_element_type=jnp.float32)
            return [whole[:, part * width : (part + 1) * width] for part in range(n_parts)]
        return [
            jnp.dot(x, weight[part], preferred_element_type=jnp.float32) for part in range(n_parts)
        ]

    def gate_step(i, carry):
        for part, gate in enumerate(product(x_all[i], gate_w)):
            opened[i, part] = gate / (1.0 + jnp.exp(-gate))
        return carry

    def up_step(i, carry):
        lines = pl.ds(pl.multiple_of(i * rows, rows), rows)
        for part, upward in enumerate(product(x_all[i], up_w)):
            outs[part][lines, :] = (opened[i, part] * upward).astype(outs[part].dtype)
        return carry

    for copy in first:
        copy.wait()
    lax.fori_loop(0, GROUP, gate_step, 0)
    for copy in second:
        copy.wait()
    lax.fori_loop(0, GROUP, up_step, 0)


def expand(me, normed, keys, weights):
    rows, depth = normed[0].shape
    n_parts = len(weights)
    width = weights[0][0].shape[-1]
    total = rows * GROUP
    n_copies = n_parts * GROUP * sum(len(entry or (0,)) for entry in keys)
    shape = (depth, n_parts * width) if width % 128 == 0 else (n_parts, depth, width)
    vmem, anywhere = pl.BlockSpec(memory_space=pltpu.VMEM), pl.BlockSpec(memory_space=pl.ANY)
    return pl.pallas_call(
        functools.partial(expand_kernel, n_parts=n_parts, keys=keys),
        in_specs=[pl.BlockSpec(memory_space=pltpu.SMEM)]
        + [anywhere] * (len(normed) + n_parts * len(keys)),
        out_specs=[vmem] * n_parts,
        out_shape=[jax.ShapeDtypeStruct((total, width), jnp.bfloat16)] * n_parts,
        scratch_shapes=[
            pltpu.VMEM((GROUP, rows, depth), jnp.bfloat16),
            pltpu.VMEM(shape, jnp.bfloat16),
            pltpu.VMEM(shape, jnp.bfloat16),
            pltpu.VMEM((GROUP, n_parts, rows, width), jnp.float32),
            pltpu.SemaphoreType.DMA((len(normed),)),
            pltpu.SemaphoreType.DMA((n_copies,)),
            pltpu.SemaphoreType.DMA((n_copies,)),
        ],
        compiler_params=pltpu.CompilerParams(vmem_limit_bytes=VMEM_LIMIT),
        cost_estimate=SHORT,
        name="gate_up",
    )(me, *normed, *[array for part in weights for array in part])


def down_kernel(me, *refs, n_parts, keys, mask):
    n_weights = n_parts * len(keys)
    act_refs, w_refs = refs[:n_parts], refs[n_parts : n_parts + n_weights]
    own, to_x, to_y, keep_x, keep_y, acts, weight, a_sems, w_sems = refs[n_parts + n_weights :]
    width = act_refs[0].shape[1]
    rows = own.shape[0]
    half = rows // 2
    packed = len(acts.shape) == 2
    copies = weight_copies(me[0], w_refs, keys, 0, weight, mask, w_sems)
    for i in range(n_parts):
        place = acts.at[:, pl.ds(i * width, width)] if packed else acts.at[i]
        copies.append(pltpu.make_async_copy(act_refs[i], place, a_sems.at[i]))
    for copy in copies:
        copy.start()
    for copy in copies:
        copy.wait()

    def sums(block):
        here = pl.ds(block * rows, rows)
        if packed:
            return dot_rows(acts[here, :], weight[...])
        return sum(dot_rows(acts[i, here, :], weight[i]) for i in range(n_parts))

    total = sums(3).astype(jnp.bfloat16)
    to_x[half:, :] = total[:half]
    to_y[half:, :] = total[half:]
    total = sums(1)
    to_x[:half, :] = total[:half].astype(jnp.bfloat16)
    keep_x[...] = total[half:]
    total = sums(2)
    to_y[:half, :] = total[half:].astype(jnp.bfloat16)
    keep_y[...] = total[:half]
    own[...] = sums(0)


def down(me, acts, keys, weights, mask):
    total, width = acts[0].shape
    n_parts = len(acts)
    columns = sum(math.prod(array.shape[:-1]) for array in weights[0])
    rows = total // GROUP
    if width % 128 == 0:
        shapes = [(total, n_parts * width), (columns, n_parts * width)]
    else:
        shapes = [(n_parts, total, width), (n_parts, columns, width)]
    outs = [(rows, jnp.float32), (rows, jnp.bfloat16), (rows, jnp.bfloat16)]
    outs += [(rows // 2, jnp.float32)] * 2
    return pl.pallas_call(
        functools.partial(down_kernel, n_parts=n_parts, keys=keys, mask=mask),
        out_shape=[jax.ShapeDtypeStruct((length, columns), dtype) for length, dtype in outs],
        in_specs=[pl.BlockSpec(memory_space=pltpu.SMEM)]
        + [pl.BlockSpec(memory_space=pl.ANY)] * (n_parts + n_parts * len(keys)),
        out_specs=[pl.BlockSpec(memory_space=pltpu.VMEM)] * 5,
        scratch_shapes=[pltpu.VMEM(shape, jnp.bfloat16) for shape in shapes]
        + [
            pltpu.SemaphoreType.DMA((n_parts,)),
            pltpu.SemaphoreType.DMA((n_parts * GROUP * sum(len(entry or (0,)) for entry in keys),)),
        ],
        compiler_params=pltpu.CompilerParams(vmem_limit_bytes=VMEM_LIMIT),
        cost_estimate=SHORT,
        name="down",
    )(me, *acts, *[array for part in weights for array in part])


def finish_kernel(upper, resid, *refs):
    out_ref = refs[-1]
    half, width = resid.shape[0] // 2, resid.shape[1] // 2
    for piece in range(2):
        own, from_x, from_y, late_x, late_y = refs[5 * piece : 5 * piece + 5]
        here = pl.ds(pl.multiple_of((upper[0] ^ piece) * width, 128), width)
        for rows, first, late in (
            (pl.ds(0, half), from_x, late_y),
            (pl.ds(half, half), from_y, late_x),
        ):
            total = resid[rows, here].astype(jnp.float32) + own[rows, :]
            total = total + first[:half, :].astype(jnp.float32) + late[...].astype(jnp.float32)
            out_ref[rows, here] = total.astype(out_ref.dtype)


def finish(upper, resid, pieces):
    vmem = pl.BlockSpec(memory_space=pltpu.VMEM)
    return pl.pallas_call(
        finish_kernel,
        in_specs=[pl.BlockSpec(memory_space=pltpu.SMEM)] + [vmem] * 11,
        out_specs=vmem,
        out_shape=jax.ShapeDtypeStruct(resid.shape, resid.dtype),
        compiler_params=pltpu.CompilerParams(vmem_limit_bytes=VMEM_LIMIT),
        cost_estimate=SHORT,
        name="finish",
    )(upper, resid, *[part for piece in pieces for part in piece])


def swap(value, axis, size, bits):
    return lax.ppermute(value, axis, [(i, i ^ bits) for i in range(size)])


def per_device(
    q_in,
    kv_in,
    prefix_kv,
    hidden_in,
    q_gain,
    k_gain,
    post_gain,
    w_out,
    w_gate,
    w_up,
    w_down_t,
    lengths,
    row_group,
    owner_block,
):
    n_req, n_mlp = lax.axis_size("req"), lax.axis_size("mlp")
    me, core = lax.axis_index("req"), lax.axis_index("mlp")
    tok_count = q_in.shape[0]
    local_groups = kv_in.shape[2] // HD

    def tie(tree):
        leaves, shape = jax.tree.flatten(tree)
        fixed = [isinstance(leaf, int) for leaf in leaves]
        held = iter(lax.optimization_barrier([x for x, f in zip(leaves, fixed) if not f]))
        return jax.tree.unflatten(shape, [x if f else next(held) for x, f in zip(leaves, fixed)])

    top = n_req // 2
    others = [1 << i for i in range(n_req.bit_length()) if 1 << i < n_req and 1 << i not in PARTNERS]
    others = others[::-1]
    seat = ((me & 1) + (me >> 2 & 1) * 2)[None]
    place, upper = me[None], (me // top)[None]

    def req(value, key):
        return swap(value, "req", n_req, key)

    def cores(part):
        return [part] + [swap(part, "mlp", n_mlp, k) for k in range(1, n_mlp)]

    def trade(parts):
        return [parts[0]] + [req(part, key) for part, key in zip(parts[1:], PARTNERS[1:])]

    def complete(arrays):
        for key in others[1:]:
            for held_key in list(arrays):
                if held_key ^ key not in arrays:
                    arrays[held_key ^ key] = req(arrays[held_key], key)
        return arrays

    def single(arrays):
        return [([key], cores(array)) for key, array in arrays.items()]

    def gather(shares, count, n_mats):
        keys, parts = [keys for keys, _ in shares], list(zip(*[parts for _, parts in shares]))
        if parts[0][0].shape[2] % 16 == 0:
            return keys, [list(part) for part in parts]
        spots = [(key ^ partner) % count for entry in keys for key in entry for partner in PARTNERS]
        spots = jnp.asarray([spots.index(i) for i in range(count)])
        spots = spots[(me ^ jnp.arange(count)) % count]
        ordered = []
        for part in parts:
            width = part[0].shape[-1]
            whole = [x.reshape(n_mats, -1, *x.shape[2:]) for x in part]
            whole = jnp.take(jnp.concatenate(whole, axis=1), spots, axis=1)
            ordered.append([whole.reshape(n_mats, -1, width)])
        return [None], ordered

    planes = [prefix_kv] + [req(prefix_kv, 4 * k) for k in range(1, n_req // 4)]
    held = jnp.stack(planes)
    slot = jnp.argsort(owner_block) ^ me
    spot = slot // 4 + slot % 4 * (n_req // 4)
    picked = lax.dynamic_slice_in_dim(spot, row_group[0] * BPG, BPG, 0)

    parts = list(cut(seat, [w_gate, w_up]))
    held, parts[3] = tie((held, parts[3]))
    open_w = merge(seat, trade(parts))
    last = others[-1]
    held = jnp.stack([held] + [req(held, k) for k in range(1, 4)])
    held = held.reshape(n_req, 2, PB, local_groups * HD)
    chosen = jnp.take(held, picked, axis=0)
    open_top, open_last = req(open_w, top), req(open_w, last)

    _, offset = slot_layout(lengths[0], tok_count)
    cosine, sine = rotation(offset + PLEN)
    start = (jnp.arange(tok_count, dtype=jnp.int32) - offset)[:, None]
    gains = q_gain[None], k_gain[None]

    chosen, cosine, sine, start = tie((chosen, cosine, sine, start))
    attn = attention(start, cosine, sine, *gains, q_in, kv_in, chosen, 0, local_groups)
    attn, w_down_t = tie((attn, w_down_t))
    down_parts = trade(cut(seat, [w_down_t]))

    own_rows = hidden_in.shape[0]
    sums = project(core[None], [attn], w_out, n_mlp)
    parts = [swap(sums[k], "mlp", n_mlp, k) for k in range(1, n_mlp)]
    resid, own_normed = normalize(hidden_in, post_gain[None], sums[0], parts)

    own_normed, open_top, open_last, down_parts = tie(
        (own_normed, open_top, open_last, down_parts)
    )

    half = own_rows // 2
    key_x, key_y = PARTNERS[1:3]
    next_x, next_y = req(own_normed, key_x), req(own_normed, key_y)
    early = {0: open_w, last: open_last, top: open_top}
    late = {key: array for key, array in complete(dict(early)).items() if key not in early}
    open_all = single({0: open_w, last: open_last})
    down_own = merge(seat, down_parts)
    next_x, next_y, open_all, late, open_top, down_own = tie(
        (next_x, next_y, open_all, late, open_top, down_own)
    )
    diag = [req(next_x[:half], key_y), req(next_y[half:], key_x)]
    open_all = open_all + single({top: open_top, **late})
    down_last = req(down_own, last)
    diag, open_all, down_own, down_last = tie((diag, open_all, down_own, down_last))
    normed = [own_normed, next_x, next_y] + diag

    acts = expand(place, normed, *gather(open_all, n_req, 2))
    down_top = req(down_own, top)
    near = single({0: down_own, last: down_last})
    acts, near = tie((acts, near))
    down_w = complete({0: down_own, last: down_last}) if n_req > 16 else {}
    near = near + single({key: v for key, v in down_w.items() if key not in (0, last)})
    parts = down(place, acts, *gather(near, top, 1), top - 1)
    parts, down_top = tie((parts, down_top))
    down_w = complete({top: down_top})
    far = {key: v for key, v in down_w.items() if key & top}

    sums = []
    for piece in range(2):
        own, to_x, to_y, keep_x, keep_y = parts
        from_x, from_y = req(to_x, key_x), req(to_y, key_y)
        late_y = (keep_y + from_x[half:].astype(jnp.float32)).astype(jnp.bfloat16)
        late_x = (keep_x + from_y[half:].astype(jnp.float32)).astype(jnp.bfloat16)
        if piece == 0:
            far, late_x, late_y = tie((far, late_x, late_y))
            parts = down(place, acts, *gather(single(far), top, 1), top - 1)
        late_y, late_x = req(late_y, key_y), req(late_x, key_x)
        if piece == 0:
            parts, late_y, late_x = tie((parts, late_y, late_x))
        sums.append([own, from_x, from_y, late_x, late_y])
    return finish(upper, resid, sums)


def solution(mesh):
    in_specs = (
        P("req", "mlp"),
        P(None, "req", "mlp"),
        P(None, "req", "mlp"),
        P(("req", "mlp"), None),
        P(),
        P(),
        P(),
        P("mlp", None),
        P("req", "mlp"),
        P("req", "mlp"),
        P("req", "mlp"),
        P("req", None),
        P("req"),
        P(),
    )
    out_specs = P(("req", "mlp"), None)
    return jax.shard_map(
        per_device, mesh=mesh, in_specs=in_specs, out_specs=out_specs, check_vma=False
    )
```

```python
import functools
import math

import jax
import jax.numpy as jnp
from jax import lax
from jax.experimental import pallas as pl
from jax.experimental.pallas import tpu as pltpu
from jax.sharding import PartitionSpec as P

HD = 128
PB = 64
PLEN = 512
BPG = 8
PARTNERS = (0, 1, 4, 5)
GROUP = len(PARTNERS)
VMEM_LIMIT = 48 * 1024 * 1024
SHORT = pl.CostEstimate(flops=1024, bytes_accessed=1024, transcendentals=0)


EPSILON = 1e-06
THETA = 1000000.0


def rotation(positions):
    half_width = HD // 2
    exponent = jnp.arange(half_width, dtype=jnp.float32) * (2.0 / HD)
    inv_freq = jnp.power(jnp.float32(THETA), -exponent)
    angles = positions.astype(jnp.float32)[:, None] * inv_freq[None, :]
    cosine, sine = jnp.cos(angles), jnp.sin(angles)
    return jnp.concatenate([cosine, cosine], axis=1), jnp.concatenate([-sine, sine], axis=1)


def slot_layout(row_lengths, tok_count):
    req_ends = jnp.cumsum(row_lengths)
    starts = req_ends - row_lengths
    slot_ids = jnp.arange(tok_count, dtype=jnp.int32)
    request = jnp.sum((slot_ids[:, None] >= req_ends[None, :]).astype(jnp.int32), axis=1)
    member = request[:, None] == jnp.arange(row_lengths.shape[0], dtype=jnp.int32)[None, :]
    offset = slot_ids - jnp.sum(jnp.where(member, starts[None, :], 0), axis=1)
    return (request, offset)


def dot_rows(left, right):
    return lax.dot_general(
        left, right, (((1,), (1,)), ((), ())), preferred_element_type=jnp.float32
    )


def attention_kernel(
    start_ref, cos_ref, sin_ref, q_gain, k_gain, q_ref, k_ref, v_ref, pk_ref, pv_ref, out_ref, bias
):
    tok_count = k_ref.shape[1]
    tile = min(256, tok_count)
    scale = math.log2(math.e) / math.sqrt(HD)

    @pl.when(pl.program_id(0) == 0)
    def _():
        keys = lax.broadcasted_iota(jnp.int32, (tok_count, tok_count), 1)
        slots = lax.broadcasted_iota(jnp.int32, (tok_count, tok_count), 0)
        seen = (keys >= start_ref[...]) & (keys <= slots)
        bias[...] = jnp.where(seen, 0.0, -1e30)

    def prepare(values, gain, rows):
        values = values.astype(jnp.float32)
        mean_sq = jnp.mean(values * values, axis=-1, keepdims=True)
        scaled = values * lax.rsqrt(mean_sq + EPSILON) * gain[...]
        turned = scaled * cos_ref[rows, :] + pltpu.roll(scaled, HD // 2, 1) * sin_ref[rows, :]
        return turned.astype(jnp.bfloat16)

    key = prepare(k_ref[0], k_gain, pl.ds(0, tok_count))
    value = v_ref[0]
    pre_key = pk_ref[...].reshape(-1, HD)
    pre_value = pv_ref[...].reshape(-1, HD)
    for head in range(q_ref.shape[1] // HD):
        lanes = pl.ds(head * HD, HD)
        for first in range(0, tok_count, tile):
            rows = pl.ds(first, tile)
            last = first + tile
            query = prepare(q_ref[rows, lanes], q_gain, rows)
            pre_w = jnp.exp2(dot_rows(query, pre_key) * scale)
            suf_w = jnp.exp2(dot_rows(query, key[:last]) * scale + bias[rows, :last])
            total = jnp.sum(pre_w, axis=-1, keepdims=True) + jnp.sum(suf_w, axis=-1, keepdims=True)
            top = jnp.dot(
                pre_w.astype(jnp.bfloat16), pre_value, preferred_element_type=jnp.float32
            ) + jnp.dot(
                suf_w.astype(jnp.bfloat16), value[:last], preferred_element_type=jnp.float32
            )
            out_ref[rows, lanes] = (top / total).astype(out_ref.dtype)


def attention(start, cosine, sine, q_gain, k_gain, q_in, kv_in, chosen, first, count):
    tok_count = q_in.shape[0]
    groups = kv_in.shape[2] // HD
    width = q_in.shape[1] // groups
    blocks = chosen.shape[0]

    def same(rows, columns):
        return pl.BlockSpec((rows, columns), lambda g: (0, 0))

    def suffix(which):
        return pl.BlockSpec((1, tok_count, HD), lambda g: (which, 0, g + first))

    def prefix(which):
        return pl.BlockSpec((blocks, 1, PB, HD), lambda g: (0, which, 0, g + first))

    keys = tok_count + PLEN
    return pl.pallas_call(
        attention_kernel,
        grid=(count,),
        in_specs=[
            same(tok_count, 1),
            same(tok_count, HD),
            same(tok_count, HD),
            same(1, HD),
            same(1, HD),
            pl.BlockSpec((tok_count, width), lambda g: (0, g + first)),
            suffix(0),
            suffix(1),
            prefix(0),
            prefix(1),
        ],
        out_specs=pl.BlockSpec((tok_count, width), lambda g: (0, g)),
        out_shape=jax.ShapeDtypeStruct((tok_count, count * width), jnp.bfloat16),
        scratch_shapes=[pltpu.VMEM((tok_count, tok_count), jnp.float32)],
        compiler_params=pltpu.CompilerParams(vmem_limit_bytes=VMEM_LIMIT),
        cost_estimate=SHORT,
        name="attention",
    )(start, cosine, sine, q_gain, k_gain, q_in, kv_in, kv_in, chosen, chosen)


def project_kernel(core, *refs, n_parts, n_mlp):
    parts, weights, outs = refs[:n_parts], refs[n_parts : 2 * n_parts], refs[2 * n_parts :]
    rows = outs[0].shape[0]
    for k in range(n_mlp - 1, -1, -1):
        part = pl.ds(pl.multiple_of((core[0] ^ k) * rows, rows), rows)
        total = 0.0
        for x, w in zip(parts, weights):
            total = total + jnp.dot(x[part, :], w[...], preferred_element_type=jnp.float32)
        outs[k][...] = total.astype(outs[k].dtype)


def project(core, parts, w_out, n_mlp):
    tok_count, depth = parts[0].shape
    columns = w_out.shape[1]
    rows, tile = tok_count // n_mlp, 512
    n_parts = len(parts)
    return pl.pallas_call(
        functools.partial(project_kernel, n_parts=n_parts, n_mlp=n_mlp),
        grid_spec=pltpu.PrefetchScalarGridSpec(
            num_scalar_prefetch=1,
            grid=(columns // tile,),
            in_specs=[pl.BlockSpec((tok_count, depth), lambda n, core: (0, 0))] * n_parts
            + [
                pl.BlockSpec((depth, tile), functools.partial(lambda i, n, core: (i, n), i))
                for i in range(n_parts)
            ],
            out_specs=[pl.BlockSpec((rows, tile), lambda n, core: (0, n))] * n_mlp,
        ),
        out_shape=[
            jax.ShapeDtypeStruct((rows, columns), jnp.bfloat16 if k else jnp.float32)
            for k in range(n_mlp)
        ],
        compiler_params=pltpu.CompilerParams(vmem_limit_bytes=VMEM_LIMIT),
        cost_estimate=SHORT,
        name="project",
    )(core, *parts, *[w_out] * n_parts)


def normalize_kernel(hidden, gain, own, *refs):
    parts, (resid_ref, low_ref, high_ref) = refs[:-3], refs[-3:]
    step, middle = pl.program_id(0), pl.num_programs(0) // 2
    total = hidden[...].astype(jnp.float32) + own[...]
    for part in parts:
        total = total + part[...].astype(jnp.float32)
    resid = total.astype(resid_ref.dtype)
    resid_ref[...] = resid
    values = resid.astype(jnp.float32)
    mean_sq = jnp.mean(values * values, axis=-1, keepdims=True)
    normed = (values * lax.rsqrt(mean_sq + EPSILON) * gain[...]).astype(low_ref.dtype)

    @pl.when(step < middle)
    def _():
        low_ref[...] = normed

    @pl.when(step >= middle)
    def _():
        high_ref[...] = normed


def normalize(hidden, gain, own, parts):
    rows, columns = hidden.shape
    tile = min(64, rows // 2)
    middle = rows // 2 // tile
    spec = pl.BlockSpec((tile, columns), lambda i: (i, 0))
    low = pl.BlockSpec((tile, columns), lambda i: (jnp.minimum(i, middle - 1), 0))
    high = pl.BlockSpec((tile, columns), lambda i: (jnp.maximum(i - middle, 0), 0))
    halves = jax.ShapeDtypeStruct((rows // 2, columns), hidden.dtype)
    return pl.pallas_call(
        normalize_kernel,
        grid=(2 * middle,),
        in_specs=[spec, pl.BlockSpec((1, columns), lambda i: (0, 0)), spec] + [spec] * len(parts),
        out_specs=[spec, low, high],
        out_shape=[jax.ShapeDtypeStruct(hidden.shape, hidden.dtype), halves, halves],
        compiler_params=pltpu.CompilerParams(vmem_limit_bytes=VMEM_LIMIT),
        cost_estimate=SHORT,
        name="normalize",
    )(hidden, gain, own, *parts)


def move_kernel(scalar, *refs, n_in, plan):
    sems = refs[-1]
    copies = [
        pltpu.make_async_copy(src, dst, sems.at[i])
        for i, (src, dst) in enumerate(plan(scalar[0], refs[:n_in], refs[n_in:-1]))
    ]
    for copy in copies:
        copy.start()
    for copy in copies:
        copy.wait()


def move(scalar, arrays, shapes, plan, n_copies, name):
    anywhere = pl.BlockSpec(memory_space=pl.ANY)
    return pl.pallas_call(
        functools.partial(move_kernel, n_in=len(arrays), plan=plan),
        in_specs=[pl.BlockSpec(memory_space=pltpu.SMEM)] + [anywhere] * len(arrays),
        out_specs=[pl.BlockSpec(memory_space=pltpu.VMEM)] * len(shapes),
        out_shape=[jax.ShapeDtypeStruct(shape, jnp.bfloat16) for shape in shapes],
        scratch_shapes=[pltpu.SemaphoreType.DMA((n_copies,))],
        compiler_params=pltpu.CompilerParams(vmem_limit_bytes=VMEM_LIMIT),
        cost_estimate=SHORT,
        name=name,
    )(scalar, *arrays)


def cut(seat, blocks):
    rows, columns = blocks[0].shape
    width = columns // GROUP
    if width % 128:
        return [
            jnp.stack(
                [lax.dynamic_slice_in_dim(x, (seat[0] ^ j) * width, width, 1) for x in blocks]
            )
            for j in range(GROUP)
        ]

    def plan(seat, sources, targets):
        return [
            (source.at[:, pl.ds(pl.multiple_of((seat ^ j) * width, 128), width)], targets[j].at[m])
            for j in range(GROUP)
            for m, source in enumerate(sources)
        ]

    shapes = [(len(blocks), rows, width)] * GROUP
    return move(seat, blocks, shapes, plan, GROUP * len(blocks), "cut")


def merge(seat, parts):
    n_mats, rows, width = parts[0].shape
    if width % 128:
        return jnp.stack(parts, axis=1)

    def plan(_, sources, targets):
        return [
            (source.at[m], targets[0].at[m, j])
            for j, source in enumerate(sources)
            for m in range(n_mats)
        ]

    shapes = [(n_mats, GROUP, rows, width)]
    return move(seat, parts, shapes, plan, GROUP * n_mats, "merge")[0]


def weight_copies(me, refs, keys, matrix, target, mask, sems):
    copies = []
    for i, ref in enumerate(refs):
        part, entry = divmod(i, len(keys))
        rows, width = ref.shape[-2:]
        packed = len(target.shape) == 2
        lanes = pl.ds(part * width, width)
        if keys[entry] is None:
            place = target.at[:, lanes] if packed else target.at[part]
            copies.append(pltpu.make_async_copy(ref.at[matrix], place, sems.at[len(copies)]))
            continue
        for k, key in enumerate(keys[entry]):
            for j, partner in enumerate(PARTNERS):
                source = (me ^ (key ^ partner)) & mask
                here = pl.ds(pl.multiple_of(source * rows, 8), rows)
                place = target.at[here, lanes] if packed else target.at[part, here]
                copies.append(pltpu.make_async_copy(ref.at[matrix * len(keys[entry]) + k, j], place, sems.at[len(copies)]))
    return copies


def expand_kernel(me, *refs, n_parts, keys):
    n_weights = n_parts * len(keys)
    x_refs, refs = refs[: 2 * GROUP], refs[2 * GROUP :]
    w_refs, outs, refs = refs[:n_weights], refs[n_weights : n_weights + n_parts], refs[n_weights + n_parts :]
    x_all, gate_w, up_w, opened, x_sems, gate_sems, up_sems = refs
    width = outs[0].shape[1]
    half, depth = x_refs[0].shape
    rows = 2 * half
    places = [x_all.at[i // 2, pl.ds(i % 2 * half, half)] for i in range(2 * GROUP)]
    first = weight_copies(me[0], w_refs, keys, 0, gate_w, -1, gate_sems)
    first += [
        pltpu.make_async_copy(x_ref, place, x_sems.at[i])
        for i, (x_ref, place) in enumerate(zip(x_refs, places))
    ]
    second = weight_copies(me[0], w_refs, keys, 1, up_w, -1, up_sems)
    for copy in first + second:
        copy.start()

    def product(x, weight):
        if len(weight.shape) == 2:
            whole = jnp.dot(x, weight[...], preferred_element_type=jnp.float32)
            return [whole[:, part * width : (part + 1) * width] for part in range(n_parts)]
        return [
            jnp.dot(x, weight[part], preferred_element_type=jnp.float32) for part in range(n_parts)
        ]

    def gate_step(i, carry):
        for part, gate in enumerate(product(x_all[i], gate_w)):
            opened[i, part] = gate / (1.0 + jnp.exp(-gate))
        return carry

    def up_step(i, carry):
        lines = pl.ds(pl.multiple_of(i * rows, rows), rows)
        for part, upward in enumerate(product(x_all[i], up_w)):
            outs[part][lines, :] = (opened[i, part] * upward).astype(outs[part].dtype)
        return carry

    for copy in first:
        copy.wait()
    lax.fori_loop(0, GROUP, gate_step, 0)
    for copy in second:
        copy.wait()
    lax.fori_loop(0, GROUP, up_step, 0)


def expand(me, normed, keys, weights):
    rows, depth = 2 * normed[0].shape[0], normed[0].shape[1]
    n_parts = len(weights)
    width = weights[0][0].shape[-1]
    total = rows * GROUP
    n_copies = n_parts * GROUP * sum(len(entry or (0,)) for entry in keys)
    shape = (depth, n_parts * width) if width % 128 == 0 else (n_parts, depth, width)
    vmem, anywhere = pl.BlockSpec(memory_space=pltpu.VMEM), pl.BlockSpec(memory_space=pl.ANY)
    return pl.pallas_call(
        functools.partial(expand_kernel, n_parts=n_parts, keys=keys),
        in_specs=[pl.BlockSpec(memory_space=pltpu.SMEM)]
        + [anywhere] * (len(normed) + n_parts * len(keys)),
        out_specs=[vmem] * n_parts,
        out_shape=[jax.ShapeDtypeStruct((total, width), jnp.bfloat16)] * n_parts,
        scratch_shapes=[
            pltpu.VMEM((GROUP, rows, depth), jnp.bfloat16),
            pltpu.VMEM(shape, jnp.bfloat16),
            pltpu.VMEM(shape, jnp.bfloat16),
            pltpu.VMEM((GROUP, n_parts, rows, width), jnp.float32),
            pltpu.SemaphoreType.DMA((len(normed),)),
            pltpu.SemaphoreType.DMA((n_copies,)),
            pltpu.SemaphoreType.DMA((n_copies,)),
        ],
        compiler_params=pltpu.CompilerParams(vmem_limit_bytes=VMEM_LIMIT),
        cost_estimate=SHORT,
        name="gate_up",
    )(me, *normed, *[array for part in weights for array in part])


def down_kernel(me, *refs, n_parts, keys, mask):
    n_weights = n_parts * len(keys)
    act_refs, w_refs = refs[:n_parts], refs[n_parts : n_parts + n_weights]
    own, to_x, to_y, keep_x, keep_y, acts, weight, a_sems, w_sems = refs[n_parts + n_weights :]
    width = act_refs[0].shape[1]
    rows = own.shape[0]
    half = rows // 2
    packed = len(acts.shape) == 2
    copies = weight_copies(me[0], w_refs, keys, 0, weight, mask, w_sems)
    for i in range(n_parts):
        place = acts.at[:, pl.ds(i * width, width)] if packed else acts.at[i]
        copies.append(pltpu.make_async_copy(act_refs[i], place, a_sems.at[i]))
    for copy in copies:
        copy.start()
    for copy in copies:
        copy.wait()

    def sums(block):
        here = pl.ds(block * rows, rows)
        if packed:
            return dot_rows(acts[here, :], weight[...])
        return sum(dot_rows(acts[i, here, :], weight[i]) for i in range(n_parts))

    total = sums(3).astype(jnp.bfloat16)
    to_x[half:, :] = total[:half]
    to_y[half:, :] = total[half:]
    total = sums(1)
    to_x[:half, :] = total[:half].astype(jnp.bfloat16)
    keep_x[...] = total[half:]
    total = sums(2)
    to_y[:half, :] = total[half:].astype(jnp.bfloat16)
    keep_y[...] = total[:half]
    own[...] = sums(0)


def down(me, acts, keys, weights, mask):
    total, width = acts[0].shape
    n_parts = len(acts)
    columns = sum(math.prod(array.shape[:-1]) for array in weights[0])
    rows = total // GROUP
    if width % 128 == 0:
        shapes = [(total, n_parts * width), (columns, n_parts * width)]
    else:
        shapes = [(n_parts, total, width), (n_parts, columns, width)]
    outs = [(rows, jnp.float32), (rows, jnp.bfloat16), (rows, jnp.bfloat16)]
    outs += [(rows // 2, jnp.float32)] * 2
    return pl.pallas_call(
        functools.partial(down_kernel, n_parts=n_parts, keys=keys, mask=mask),
        out_shape=[jax.ShapeDtypeStruct((length, columns), dtype) for length, dtype in outs],
        in_specs=[pl.BlockSpec(memory_space=pltpu.SMEM)]
        + [pl.BlockSpec(memory_space=pl.ANY)] * (n_parts + n_parts * len(keys)),
        out_specs=[pl.BlockSpec(memory_space=pltpu.VMEM)] * 5,
        scratch_shapes=[pltpu.VMEM(shape, jnp.bfloat16) for shape in shapes]
        + [
            pltpu.SemaphoreType.DMA((n_parts,)),
            pltpu.SemaphoreType.DMA((n_parts * GROUP * sum(len(entry or (0,)) for entry in keys),)),
        ],
        compiler_params=pltpu.CompilerParams(vmem_limit_bytes=VMEM_LIMIT),
        cost_estimate=SHORT,
        name="down",
    )(me, *acts, *[array for part in weights for array in part])


def finish_kernel(upper, resid, *refs):
    out_ref = refs[-1]
    half, width = resid.shape[0] // 2, resid.shape[1] // 2
    for piece in range(2):
        own, from_x, from_y, late_x, late_y = refs[5 * piece : 5 * piece + 5]
        here = pl.ds(pl.multiple_of((upper[0] ^ piece) * width, 128), width)
        for rows, first, late in (
            (pl.ds(0, half), from_x, late_y),
            (pl.ds(half, half), from_y, late_x),
        ):
            total = resid[rows, here].astype(jnp.float32) + own[rows, :]
            total = total + first[:half, :].astype(jnp.float32) + late[...].astype(jnp.float32)
            out_ref[rows, here] = total.astype(out_ref.dtype)


def finish(upper, resid, pieces):
    vmem = pl.BlockSpec(memory_space=pltpu.VMEM)
    return pl.pallas_call(
        finish_kernel,
        in_specs=[pl.BlockSpec(memory_space=pltpu.SMEM)] + [vmem] * 11,
        out_specs=vmem,
        out_shape=jax.ShapeDtypeStruct(resid.shape, resid.dtype),
        compiler_params=pltpu.CompilerParams(vmem_limit_bytes=VMEM_LIMIT),
        cost_estimate=SHORT,
        name="finish",
    )(upper, resid, *[part for piece in pieces for part in piece])


def swap(value, axis, size, bits):
    return lax.ppermute(value, axis, [(i, i ^ bits) for i in range(size)])


def per_device(
    q_in,
    kv_in,
    prefix_kv,
    hidden_in,
    q_gain,
    k_gain,
    post_gain,
    w_out,
    w_gate,
    w_up,
    w_down_t,
    lengths,
    row_group,
    owner_block,
):
    n_req, n_mlp = lax.axis_size("req"), lax.axis_size("mlp")
    me, core = lax.axis_index("req"), lax.axis_index("mlp")
    tok_count = q_in.shape[0]
    local_groups = kv_in.shape[2] // HD

    def tie(tree):
        leaves, shape = jax.tree.flatten(tree)
        fixed = [isinstance(leaf, int) for leaf in leaves]
        held = iter(lax.optimization_barrier([x for x, f in zip(leaves, fixed) if not f]))
        return jax.tree.unflatten(shape, [x if f else next(held) for x, f in zip(leaves, fixed)])

    top = n_req // 2
    others = [1 << i for i in range(n_req.bit_length()) if 1 << i < n_req and 1 << i not in PARTNERS]
    others = others[::-1]
    seat = ((me & 1) + (me >> 2 & 1) * 2)[None]
    place, upper = me[None], (me // top)[None]

    def req(value, key):
        return swap(value, "req", n_req, key)

    def cores(part):
        return [part] + [swap(part, "mlp", n_mlp, k) for k in range(1, n_mlp)]

    def trade(parts):
        return [parts[0]] + [req(part, key) for part, key in zip(parts[1:], PARTNERS[1:])]

    def complete(arrays):
        for key in others[1:]:
            for held_key in list(arrays):
                if held_key ^ key not in arrays:
                    arrays[held_key ^ key] = req(arrays[held_key], key)
        return arrays

    def single(arrays):
        return [([key], cores(array)) for key, array in arrays.items()]

    def gather(shares, count, n_mats):
        keys, parts = [keys for keys, _ in shares], list(zip(*[parts for _, parts in shares]))
        if parts[0][0].shape[2] % 16 == 0:
            return keys, [list(part) for part in parts]
        spots = [(key ^ partner) % count for entry in keys for key in entry for partner in PARTNERS]
        spots = jnp.asarray([spots.index(i) for i in range(count)])
        spots = spots[(me ^ jnp.arange(count)) % count]
        ordered = []
        for part in parts:
            width = part[0].shape[-1]
            whole = [x.reshape(n_mats, -1, *x.shape[2:]) for x in part]
            whole = jnp.take(jnp.concatenate(whole, axis=1), spots, axis=1)
            ordered.append([whole.reshape(n_mats, -1, width)])
        return [None], ordered

    planes = [prefix_kv] + [req(prefix_kv, 4 * k) for k in range(1, n_req // 4)]
    held = jnp.stack(planes)
    slot = jnp.argsort(owner_block) ^ me
    spot = slot // 4 + slot % 4 * (n_req // 4)
    picked = lax.dynamic_slice_in_dim(spot, row_group[0] * BPG, BPG, 0)

    parts = list(cut(seat, [w_gate, w_up]))
    held, parts[3] = tie((held, parts[3]))
    open_w = merge(seat, trade(parts))
    open_w, w_down_t = tie((open_w, w_down_t))
    last = others[-1]
    held = jnp.stack([held] + [req(held, k) for k in range(1, 4)])
    held = held.reshape(n_req, 2, PB, local_groups * HD)
    chosen = jnp.take(held, picked, axis=0)
    open_top, open_last = req(open_w, top), req(open_w, last)

    _, offset = slot_layout(lengths[0], tok_count)
    cosine, sine = rotation(offset + PLEN)
    start = (jnp.arange(tok_count, dtype=jnp.int32) - offset)[:, None]
    gains = q_gain[None], k_gain[None]

    chosen, cosine, sine, start = tie((chosen, cosine, sine, start))
    attn = attention(start, cosine, sine, *gains, q_in, kv_in, chosen, 0, local_groups)
    attn, down_parts = tie((attn, trade(cut(seat, [w_down_t]))))
    down_own = merge(seat, down_parts)
    down_last = req(down_own, last)

    own_rows = hidden_in.shape[0]
    sums = project(core[None], [attn], w_out, n_mlp)
    parts = [swap(sums[k], "mlp", n_mlp, k) for k in range(1, n_mlp)]
    resid, *own_normed = normalize(hidden_in, post_gain[None], sums[0], parts)

    own_normed, open_top, open_last, down_own, down_last = tie(
        (own_normed, open_top, open_last, down_own, down_last)
    )

    half = own_rows // 2
    key_x, key_y = PARTNERS[1:3]
    low, high = own_normed
    low_x, high_y = req(low, key_x), req(high, key_y)
    late = complete({0: open_w, last: open_last, top: open_top})
    late = {key: late[key] for key in late if key not in (0, last, top)}
    open_all = single({0: open_w})
    low_x, high_y = tie((low_x, high_y))
    high_x, low_y = req(high, key_x), req(low, key_y)
    diag = [req(low_x, key_y), req(high_y, key_x)]
    open_all = open_all + single({last: open_last, top: open_top})
    diag, high_x, low_y, open_all, late, down_own, down_last = tie(
        (diag, high_x, low_y, open_all, late, down_own, down_last)
    )
    open_all = open_all + single(late)
    normed = [low, high, low_x, high_x, low_y, high_y] + diag

    acts = expand(place, normed, *gather(open_all, n_req, 2))
    down_top = req(down_own, top)
    near = single({0: down_own, last: down_last})
    acts, near = tie((acts, near))
    down_w = complete({0: down_own, last: down_last}) if n_req > 16 else {}
    near = near + single({key: v for key, v in down_w.items() if key not in (0, last)})
    parts = down(place, acts, *gather(near, top, 1), top - 1)
    parts, down_top = tie((parts, down_top))
    down_w = complete({top: down_top})
    far = {key: v for key, v in down_w.items() if key & top}

    sums = []
    for piece in range(2):
        own, to_x, to_y, keep_x, keep_y = parts
        from_x, from_y = req(to_x, key_x), req(to_y, key_y)
        late_y = (keep_y + from_x[half:].astype(jnp.float32)).astype(jnp.bfloat16)
        late_x = (keep_x + from_y[half:].astype(jnp.float32)).astype(jnp.bfloat16)
        if piece == 0:
            far, late_x, late_y = tie((far, late_x, late_y))
            parts = down(place, acts, *gather(single(far), top, 1), top - 1)
        late_y, late_x = req(late_y, key_y), req(late_x, key_x)
        if piece == 0:
            parts, late_y, late_x = tie((parts, late_y, late_x))
        sums.append([own, from_x, from_y, late_x, late_y])
    return finish(upper, resid, sums)


def solution(mesh):
    in_specs = (
        P("req", "mlp"),
        P(None, "req", "mlp"),
        P(None, "req", "mlp"),
        P(("req", "mlp"), None),
        P(),
        P(),
        P(),
        P("mlp", None),
        P("req", "mlp"),
        P("req", "mlp"),
        P("req", "mlp"),
        P("req", None),
        P("req"),
        P(),
    )
    out_specs = P(("req", "mlp"), None)
    return jax.shard_map(
        per_device, mesh=mesh, in_specs=in_specs, out_specs=out_specs, check_vma=False
    )
```

```python
import functools
import math

import jax
import jax.numpy as jnp
from jax import lax
from jax.experimental import pallas as pl
from jax.experimental.pallas import tpu as pltpu
from jax.sharding import PartitionSpec as P

HD = 128
PB = 64
PLEN = 512
BPG = 8
PARTNERS = (0, 1, 4, 5)
GROUP = len(PARTNERS)
VMEM_LIMIT = 48 * 1024 * 1024
SHORT = pl.CostEstimate(flops=1024, bytes_accessed=1024, transcendentals=0)


EPSILON = 1e-06
THETA = 1000000.0


def rotation(positions):
    half_width = HD // 2
    exponent = jnp.arange(half_width, dtype=jnp.float32) * (2.0 / HD)
    inv_freq = jnp.power(jnp.float32(THETA), -exponent)
    angles = positions.astype(jnp.float32)[:, None] * inv_freq[None, :]
    cosine, sine = jnp.cos(angles), jnp.sin(angles)
    return jnp.concatenate([cosine, cosine], axis=1), jnp.concatenate([-sine, sine], axis=1)


def slot_layout(row_lengths, tok_count):
    req_ends = jnp.cumsum(row_lengths)
    starts = req_ends - row_lengths
    slot_ids = jnp.arange(tok_count, dtype=jnp.int32)
    request = jnp.sum((slot_ids[:, None] >= req_ends[None, :]).astype(jnp.int32), axis=1)
    member = request[:, None] == jnp.arange(row_lengths.shape[0], dtype=jnp.int32)[None, :]
    offset = slot_ids - jnp.sum(jnp.where(member, starts[None, :], 0), axis=1)
    return (request, offset)


def dot_rows(left, right):
    return lax.dot_general(
        left, right, (((1,), (1,)), ((), ())), preferred_element_type=jnp.float32
    )


def attention_kernel(
    start_ref, cos_ref, sin_ref, q_gain, k_gain, q_ref, k_ref, v_ref, pk_ref, pv_ref, out_ref, bias
):
    tok_count = k_ref.shape[1]
    tile = min(256, tok_count)
    scale = math.log2(math.e) / math.sqrt(HD)

    @pl.when(pl.program_id(0) == 0)
    def _():
        keys = lax.broadcasted_iota(jnp.int32, (tok_count, tok_count), 1)
        slots = lax.broadcasted_iota(jnp.int32, (tok_count, tok_count), 0)
        seen = (keys >= start_ref[...]) & (keys <= slots)
        bias[...] = jnp.where(seen, 0.0, -1e30)

    def prepare(values, gain, rows):
        values = values.astype(jnp.float32)
        mean_sq = jnp.mean(values * values, axis=-1, keepdims=True)
        scaled = values * lax.rsqrt(mean_sq + EPSILON) * gain[...]
        turned = scaled * cos_ref[rows, :] + pltpu.roll(scaled, HD // 2, 1) * sin_ref[rows, :]
        return turned.astype(jnp.bfloat16)

    key = prepare(k_ref[0], k_gain, pl.ds(0, tok_count))
    value = v_ref[0]
    pre_key = pk_ref[...].reshape(-1, HD)
    pre_value = pv_ref[...].reshape(-1, HD)
    for head in range(q_ref.shape[1] // HD):
        lanes = pl.ds(head * HD, HD)
        for first in range(0, tok_count, tile):
            rows = pl.ds(first, tile)
            last = first + tile
            query = prepare(q_ref[rows, lanes], q_gain, rows)
            pre_w = jnp.exp2(dot_rows(query, pre_key) * scale)
            suf_w = jnp.exp2(dot_rows(query, key[:last]) * scale + bias[rows, :last])
            total = jnp.sum(pre_w, axis=-1, keepdims=True) + jnp.sum(suf_w, axis=-1, keepdims=True)
            top = jnp.dot(
                pre_w.astype(jnp.bfloat16), pre_value, preferred_element_type=jnp.float32
            ) + jnp.dot(
                suf_w.astype(jnp.bfloat16), value[:last], preferred_element_type=jnp.float32
            )
            out_ref[rows, lanes] = (top / total).astype(out_ref.dtype)


def attention(start, cosine, sine, q_gain, k_gain, q_in, kv_in, chosen, first, count):
    tok_count = q_in.shape[0]
    groups = kv_in.shape[2] // HD
    width = q_in.shape[1] // groups
    blocks = chosen.shape[0]

    def same(rows, columns):
        return pl.BlockSpec((rows, columns), lambda g: (0, 0))

    def suffix(which):
        return pl.BlockSpec((1, tok_count, HD), lambda g: (which, 0, g + first))

    def prefix(which):
        return pl.BlockSpec((blocks, 1, PB, HD), lambda g: (0, which, 0, g + first))

    keys = tok_count + PLEN
    return pl.pallas_call(
        attention_kernel,
        grid=(count,),
        in_specs=[
            same(tok_count, 1),
            same(tok_count, HD),
            same(tok_count, HD),
            same(1, HD),
            same(1, HD),
            pl.BlockSpec((tok_count, width), lambda g: (0, g + first)),
            suffix(0),
            suffix(1),
            prefix(0),
            prefix(1),
        ],
        out_specs=pl.BlockSpec((tok_count, width), lambda g: (0, g)),
        out_shape=jax.ShapeDtypeStruct((tok_count, count * width), jnp.bfloat16),
        scratch_shapes=[pltpu.VMEM((tok_count, tok_count), jnp.float32)],
        compiler_params=pltpu.CompilerParams(vmem_limit_bytes=VMEM_LIMIT),
        cost_estimate=SHORT,
        name="attention",
    )(start, cosine, sine, q_gain, k_gain, q_in, kv_in, kv_in, chosen, chosen)


def project_kernel(core, *refs, n_parts, n_mlp):
    parts, weights, outs = refs[:n_parts], refs[n_parts : 2 * n_parts], refs[2 * n_parts :]
    rows = outs[0].shape[0]
    for k in range(n_mlp - 1, -1, -1):
        part = pl.ds(pl.multiple_of((core[0] ^ k) * rows, rows), rows)
        total = 0.0
        for x, w in zip(parts, weights):
            total = total + jnp.dot(x[part, :], w[...], preferred_element_type=jnp.float32)
        outs[k][...] = total.astype(outs[k].dtype)


def project(core, parts, w_out, n_mlp):
    tok_count, depth = parts[0].shape
    columns = w_out.shape[1]
    rows, tile = tok_count // n_mlp, 512
    n_parts = len(parts)
    return pl.pallas_call(
        functools.partial(project_kernel, n_parts=n_parts, n_mlp=n_mlp),
        grid_spec=pltpu.PrefetchScalarGridSpec(
            num_scalar_prefetch=1,
            grid=(columns // tile,),
            in_specs=[pl.BlockSpec((tok_count, depth), lambda n, core: (0, 0))] * n_parts
            + [
                pl.BlockSpec((depth, tile), functools.partial(lambda i, n, core: (i, n), i))
                for i in range(n_parts)
            ],
            out_specs=[pl.BlockSpec((rows, tile), lambda n, core: (0, n))] * n_mlp,
        ),
        out_shape=[
            jax.ShapeDtypeStruct((rows, columns), jnp.bfloat16 if k else jnp.float32)
            for k in range(n_mlp)
        ],
        compiler_params=pltpu.CompilerParams(vmem_limit_bytes=VMEM_LIMIT),
        cost_estimate=SHORT,
        name="project",
    )(core, *parts, *[w_out] * n_parts)


def normalize_kernel(hidden, gain, own, *refs):
    parts, (resid_ref, low_ref, high_ref) = refs[:-3], refs[-3:]
    step, middle = pl.program_id(0), pl.num_programs(0) // 2
    total = hidden[...].astype(jnp.float32) + own[...]
    for part in parts:
        total = total + part[...].astype(jnp.float32)
    resid = total.astype(resid_ref.dtype)
    resid_ref[...] = resid
    values = resid.astype(jnp.float32)
    mean_sq = jnp.mean(values * values, axis=-1, keepdims=True)
    normed = (values * lax.rsqrt(mean_sq + EPSILON) * gain[...]).astype(low_ref.dtype)

    @pl.when(step < middle)
    def _():
        low_ref[...] = normed

    @pl.when(step >= middle)
    def _():
        high_ref[...] = normed


def normalize(hidden, gain, own, parts):
    rows, columns = hidden.shape
    tile = min(64, rows // 2)
    middle = rows // 2 // tile
    spec = pl.BlockSpec((tile, columns), lambda i: (i, 0))
    low = pl.BlockSpec((tile, columns), lambda i: (jnp.minimum(i, middle - 1), 0))
    high = pl.BlockSpec((tile, columns), lambda i: (jnp.maximum(i - middle, 0), 0))
    halves = jax.ShapeDtypeStruct((rows // 2, columns), hidden.dtype)
    return pl.pallas_call(
        normalize_kernel,
        grid=(2 * middle,),
        in_specs=[spec, pl.BlockSpec((1, columns), lambda i: (0, 0)), spec] + [spec] * len(parts),
        out_specs=[spec, low, high],
        out_shape=[jax.ShapeDtypeStruct(hidden.shape, hidden.dtype), halves, halves],
        compiler_params=pltpu.CompilerParams(vmem_limit_bytes=VMEM_LIMIT),
        cost_estimate=SHORT,
        name="normalize",
    )(hidden, gain, own, *parts)


def move_kernel(scalar, *refs, n_in, plan):
    sems = refs[-1]
    copies = [
        pltpu.make_async_copy(src, dst, sems.at[i])
        for i, (src, dst) in enumerate(plan(scalar[0], refs[:n_in], refs[n_in:-1]))
    ]
    for copy in copies:
        copy.start()
    for copy in copies:
        copy.wait()


def move(scalar, arrays, shapes, plan, n_copies, name):
    anywhere = pl.BlockSpec(memory_space=pl.ANY)
    return pl.pallas_call(
        functools.partial(move_kernel, n_in=len(arrays), plan=plan),
        in_specs=[pl.BlockSpec(memory_space=pltpu.SMEM)] + [anywhere] * len(arrays),
        out_specs=[pl.BlockSpec(memory_space=pltpu.VMEM)] * len(shapes),
        out_shape=[jax.ShapeDtypeStruct(shape, jnp.bfloat16) for shape in shapes],
        scratch_shapes=[pltpu.SemaphoreType.DMA((n_copies,))],
        compiler_params=pltpu.CompilerParams(vmem_limit_bytes=VMEM_LIMIT),
        cost_estimate=SHORT,
        name=name,
    )(scalar, *arrays)


def cut(seat, blocks):
    rows, columns = blocks[0].shape
    width = columns // GROUP
    if width % 128:
        return [
            jnp.stack(
                [lax.dynamic_slice_in_dim(x, (seat[0] ^ j) * width, width, 1) for x in blocks]
            )
            for j in range(GROUP)
        ]

    def plan(seat, sources, targets):
        return [
            (source.at[:, pl.ds(pl.multiple_of((seat ^ j) * width, 128), width)], targets[j].at[m])
            for j in range(GROUP)
            for m, source in enumerate(sources)
        ]

    shapes = [(len(blocks), rows, width)] * GROUP
    return move(seat, blocks, shapes, plan, GROUP * len(blocks), "cut")


def merge(seat, parts):
    n_mats, rows, width = parts[0].shape
    if width % 128:
        return jnp.stack(parts, axis=1)

    def plan(_, sources, targets):
        return [
            (source.at[m], targets[0].at[m, j])
            for j, source in enumerate(sources)
            for m in range(n_mats)
        ]

    shapes = [(n_mats, GROUP, rows, width)]
    return move(seat, parts, shapes, plan, GROUP * n_mats, "merge")[0]


def weight_copies(me, refs, keys, matrix, target, mask, sems):
    copies = []
    for i, ref in enumerate(refs):
        part, entry = divmod(i, len(keys))
        rows, width = ref.shape[-2:]
        packed = len(target.shape) == 2
        lanes = pl.ds(part * width, width)
        if keys[entry] is None:
            place = target.at[:, lanes] if packed else target.at[part]
            copies.append(pltpu.make_async_copy(ref.at[matrix], place, sems.at[len(copies)]))
            continue
        for k, key in enumerate(keys[entry]):
            for j, partner in enumerate(PARTNERS):
                source = (me ^ (key ^ partner)) & mask
                here = pl.ds(pl.multiple_of(source * rows, 8), rows)
                place = target.at[here, lanes] if packed else target.at[part, here]
                copies.append(pltpu.make_async_copy(ref.at[matrix * len(keys[entry]) + k, j], place, sems.at[len(copies)]))
    return copies


def expand_kernel(me, *refs, n_parts, keys):
    n_weights = n_parts * len(keys)
    x_refs, refs = refs[: 2 * GROUP], refs[2 * GROUP :]
    w_refs, outs, refs = refs[:n_weights], refs[n_weights : n_weights + n_parts], refs[n_weights + n_parts :]
    x_all, gate_w, up_w, opened, x_sems, gate_sems, up_sems = refs
    width = outs[0].shape[1]
    half, depth = x_refs[0].shape
    rows = 4 * half
    places = [x_all.at[i // 4, pl.ds(i % 4 * half, half)] for i in range(2 * GROUP)]
    first = weight_copies(me[0], w_refs, keys, 0, gate_w, -1, gate_sems)
    first += [
        pltpu.make_async_copy(x_ref, place, x_sems.at[i])
        for i, (x_ref, place) in enumerate(zip(x_refs, places))
    ]
    second = weight_copies(me[0], w_refs, keys, 1, up_w, -1, up_sems)
    for copy in first + second:
        copy.start()

    def product(x, weight):
        if len(weight.shape) == 2:
            whole = jnp.dot(x, weight[...], preferred_element_type=jnp.float32)
            return [whole[:, part * width : (part + 1) * width] for part in range(n_parts)]
        return [
            jnp.dot(x, weight[part], preferred_element_type=jnp.float32) for part in range(n_parts)
        ]

    def gate_step(i, carry):
        for part, gate in enumerate(product(x_all[i], gate_w)):
            opened[i, part] = gate / (1.0 + jnp.exp(-gate))
        return carry

    def up_step(i, carry):
        lines = pl.ds(pl.multiple_of(i * rows, rows), rows)
        for part, upward in enumerate(product(x_all[i], up_w)):
            outs[part][lines, :] = (opened[i, part] * upward).astype(outs[part].dtype)
        return carry

    for copy in first:
        copy.wait()
    lax.fori_loop(0, GROUP // 2, gate_step, 0)
    for copy in second:
        copy.wait()
    lax.fori_loop(0, GROUP // 2, up_step, 0)


def expand(me, normed, keys, weights):
    rows, depth = 2 * normed[0].shape[0], normed[0].shape[1]
    n_parts = len(weights)
    width = weights[0][0].shape[-1]
    total = rows * GROUP
    n_copies = n_parts * GROUP * sum(len(entry or (0,)) for entry in keys)
    shape = (depth, n_parts * width) if width % 128 == 0 else (n_parts, depth, width)
    vmem, anywhere = pl.BlockSpec(memory_space=pltpu.VMEM), pl.BlockSpec(memory_space=pl.ANY)
    return pl.pallas_call(
        functools.partial(expand_kernel, n_parts=n_parts, keys=keys),
        in_specs=[pl.BlockSpec(memory_space=pltpu.SMEM)]
        + [anywhere] * (len(normed) + n_parts * len(keys)),
        out_specs=[vmem] * n_parts,
        out_shape=[jax.ShapeDtypeStruct((total, width), jnp.bfloat16)] * n_parts,
        scratch_shapes=[
            pltpu.VMEM((GROUP // 2, 2 * rows, depth), jnp.bfloat16),
            pltpu.VMEM(shape, jnp.bfloat16),
            pltpu.VMEM(shape, jnp.bfloat16),
            pltpu.VMEM((GROUP // 2, n_parts, 2 * rows, width), jnp.float32),
            pltpu.SemaphoreType.DMA((len(normed),)),
            pltpu.SemaphoreType.DMA((n_copies,)),
            pltpu.SemaphoreType.DMA((n_copies,)),
        ],
        compiler_params=pltpu.CompilerParams(vmem_limit_bytes=VMEM_LIMIT),
        cost_estimate=SHORT,
        name="gate_up",
    )(me, *normed, *[array for part in weights for array in part])


def down_kernel(me, *refs, n_parts, keys, mask):
    n_weights = n_parts * len(keys)
    act_refs, w_refs = refs[:n_parts], refs[n_parts : n_parts + n_weights]
    own, to_x, to_y, keep_x, keep_y, acts, weight, a_sems, w_sems = refs[n_parts + n_weights :]
    width = act_refs[0].shape[1]
    rows = own.shape[0]
    half = rows // 2
    packed = len(acts.shape) == 2
    copies = weight_copies(me[0], w_refs, keys, 0, weight, mask, w_sems)
    for i in range(n_parts):
        place = acts.at[:, pl.ds(i * width, width)] if packed else acts.at[i]
        copies.append(pltpu.make_async_copy(act_refs[i], place, a_sems.at[i]))
    for copy in copies:
        copy.start()
    for copy in copies:
        copy.wait()

    def sums(block):
        here = pl.ds(block * rows, 2 * rows)
        if packed:
            total = dot_rows(acts[here, :], weight[...])
        else:
            total = sum(dot_rows(acts[i, here, :], weight[i]) for i in range(n_parts))
        return total[:rows], total[rows:]

    near, far = sums(2)
    to_x[half:, :] = far[:half].astype(jnp.bfloat16)
    to_y[half:, :] = far[half:].astype(jnp.bfloat16)
    to_y[:half, :] = near[half:].astype(jnp.bfloat16)
    keep_y[...] = near[:half]
    near, far = sums(0)
    to_x[:half, :] = far[:half].astype(jnp.bfloat16)
    keep_x[...] = far[half:]
    own[...] = near


def down(me, acts, keys, weights, mask):
    total, width = acts[0].shape
    n_parts = len(acts)
    columns = sum(math.prod(array.shape[:-1]) for array in weights[0])
    rows = total // GROUP
    if width % 128 == 0:
        shapes = [(total, n_parts * width), (columns, n_parts * width)]
    else:
        shapes = [(n_parts, total, width), (n_parts, columns, width)]
    outs = [(rows, jnp.float32), (rows, jnp.bfloat16), (rows, jnp.bfloat16)]
    outs += [(rows // 2, jnp.float32)] * 2
    return pl.pallas_call(
        functools.partial(down_kernel, n_parts=n_parts, keys=keys, mask=mask),
        out_shape=[jax.ShapeDtypeStruct((length, columns), dtype) for length, dtype in outs],
        in_specs=[pl.BlockSpec(memory_space=pltpu.SMEM)]
        + [pl.BlockSpec(memory_space=pl.ANY)] * (n_parts + n_parts * len(keys)),
        out_specs=[pl.BlockSpec(memory_space=pltpu.VMEM)] * 5,
        scratch_shapes=[pltpu.VMEM(shape, jnp.bfloat16) for shape in shapes]
        + [
            pltpu.SemaphoreType.DMA((n_parts,)),
            pltpu.SemaphoreType.DMA((n_parts * GROUP * sum(len(entry or (0,)) for entry in keys),)),
        ],
        compiler_params=pltpu.CompilerParams(vmem_limit_bytes=VMEM_LIMIT),
        cost_estimate=SHORT,
        name="down",
    )(me, *acts, *[array for part in weights for array in part])


def finish_kernel(upper, resid, *refs):
    out_ref = refs[-1]
    half, width = resid.shape[0] // 2, resid.shape[1] // 2
    for piece in range(2):
        own, from_x, from_y, late_x, late_y = refs[5 * piece : 5 * piece + 5]
        here = pl.ds(pl.multiple_of((upper[0] ^ piece) * width, 128), width)
        for rows, first, late in (
            (pl.ds(0, half), from_x, late_y),
            (pl.ds(half, half), from_y, late_x),
        ):
            total = resid[rows, here].astype(jnp.float32) + own[rows, :]
            total = total + first[:half, :].astype(jnp.float32) + late[...].astype(jnp.float32)
            out_ref[rows, here] = total.astype(out_ref.dtype)


def finish(upper, resid, pieces):
    vmem = pl.BlockSpec(memory_space=pltpu.VMEM)
    return pl.pallas_call(
        finish_kernel,
        in_specs=[pl.BlockSpec(memory_space=pltpu.SMEM)] + [vmem] * 11,
        out_specs=vmem,
        out_shape=jax.ShapeDtypeStruct(resid.shape, resid.dtype),
        compiler_params=pltpu.CompilerParams(vmem_limit_bytes=VMEM_LIMIT),
        cost_estimate=SHORT,
        name="finish",
    )(upper, resid, *[part for piece in pieces for part in piece])


def swap(value, axis, size, bits):
    return lax.ppermute(value, axis, [(i, i ^ bits) for i in range(size)])


def per_device(
    q_in,
    kv_in,
    prefix_kv,
    hidden_in,
    q_gain,
    k_gain,
    post_gain,
    w_out,
    w_gate,
    w_up,
    w_down_t,
    lengths,
    row_group,
    owner_block,
):
    n_req, n_mlp = lax.axis_size("req"), lax.axis_size("mlp")
    me, core = lax.axis_index("req"), lax.axis_index("mlp")
    tok_count = q_in.shape[0]
    local_groups = kv_in.shape[2] // HD

    def tie(tree):
        leaves, shape = jax.tree.flatten(tree)
        fixed = [isinstance(leaf, int) for leaf in leaves]
        held = iter(lax.optimization_barrier([x for x, f in zip(leaves, fixed) if not f]))
        return jax.tree.unflatten(shape, [x if f else next(held) for x, f in zip(leaves, fixed)])

    top = n_req // 2
    others = [1 << i for i in range(n_req.bit_length()) if 1 << i < n_req and 1 << i not in PARTNERS]
    others = others[::-1]
    seat = ((me & 1) + (me >> 2 & 1) * 2)[None]
    place, upper = me[None], (me // top)[None]

    def req(value, key):
        return swap(value, "req", n_req, key)

    def cores(part):
        return [part] + [swap(part, "mlp", n_mlp, k) for k in range(1, n_mlp)]

    def trade(parts):
        return [parts[0]] + [req(part, key) for part, key in zip(parts[1:], PARTNERS[1:])]

    def complete(arrays):
        for key in others[1:]:
            for held_key in list(arrays):
                if held_key ^ key not in arrays:
                    arrays[held_key ^ key] = req(arrays[held_key], key)
        return arrays

    def single(arrays):
        return [([key], cores(array)) for key, array in arrays.items()]

    def gather(shares, count, n_mats):
        keys, parts = [keys for keys, _ in shares], list(zip(*[parts for _, parts in shares]))
        if parts[0][0].shape[2] % 16 == 0:
            return keys, [list(part) for part in parts]
        spots = [(key ^ partner) % count for entry in keys for key in entry for partner in PARTNERS]
        spots = jnp.asarray([spots.index(i) for i in range(count)])
        spots = spots[(me ^ jnp.arange(count)) % count]
        ordered = []
        for part in parts:
            width = part[0].shape[-1]
            whole = [x.reshape(n_mats, -1, *x.shape[2:]) for x in part]
            whole = jnp.take(jnp.concatenate(whole, axis=1), spots, axis=1)
            ordered.append([whole.reshape(n_mats, -1, width)])
        return [None], ordered

    planes = [prefix_kv] + [req(prefix_kv, 4 * k) for k in range(1, n_req // 4)]
    held = jnp.stack(planes)
    slot = jnp.argsort(owner_block) ^ me
    spot = slot // 4 + slot % 4 * (n_req // 4)
    picked = lax.dynamic_slice_in_dim(spot, row_group[0] * BPG, BPG, 0)

    parts = list(cut(seat, [w_gate, w_up]))
    held, parts[3] = tie((held, parts[3]))
    open_w = merge(seat, trade(parts))
    open_w, w_down_t = tie((open_w, w_down_t))
    last = others[-1]
    held = jnp.stack([held] + [req(held, k) for k in range(1, 4)])
    held = held.reshape(n_req, 2, PB, local_groups * HD)
    chosen = jnp.take(held, picked, axis=0)
    open_top, open_last = req(open_w, top), req(open_w, last)

    _, offset = slot_layout(lengths[0], tok_count)
    cosine, sine = rotation(offset + PLEN)
    start = (jnp.arange(tok_count, dtype=jnp.int32) - offset)[:, None]
    gains = q_gain[None], k_gain[None]

    chosen, cosine, sine, start = tie((chosen, cosine, sine, start))
    attn = attention(start, cosine, sine, *gains, q_in, kv_in, chosen, 0, local_groups)
    attn, down_parts = tie((attn, trade(cut(seat, [w_down_t]))))
    down_own = merge(seat, down_parts)
    down_last = req(down_own, last)

    own_rows = hidden_in.shape[0]
    sums = project(core[None], [attn], w_out, n_mlp)
    parts = [swap(sums[k], "mlp", n_mlp, k) for k in range(1, n_mlp)]
    resid, *own_normed = normalize(hidden_in, post_gain[None], sums[0], parts)

    own_normed, open_top, open_last, down_own, down_last = tie(
        (own_normed, open_top, open_last, down_own, down_last)
    )

    half = own_rows // 2
    key_x, key_y = PARTNERS[1:3]
    low, high = own_normed
    low_x, high_y = req(low, key_x), req(high, key_y)
    late = complete({0: open_w, last: open_last, top: open_top})
    late = {key: late[key] for key in late if key not in (0, last, top)}
    open_all = single({0: open_w})
    low_x, high_y = tie((low_x, high_y))
    high_x, low_y = req(high, key_x), req(low, key_y)
    diag = [req(low_x, key_y), req(high_y, key_x)]
    open_all = open_all + single({last: open_last, top: open_top})
    diag, high_x, low_y, open_all, late, down_own, down_last = tie(
        (diag, high_x, low_y, open_all, late, down_own, down_last)
    )
    open_all = open_all + single(late)
    normed = [low, high, low_x, high_x, low_y, high_y] + diag

    acts = expand(place, normed, *gather(open_all, n_req, 2))
    down_top = req(down_own, top)
    near = single({0: down_own, last: down_last})
    acts, near = tie((acts, near))
    down_w = complete({0: down_own, last: down_last}) if n_req > 16 else {}
    near = near + single({key: v for key, v in down_w.items() if key not in (0, last)})
    parts = down(place, acts, *gather(near, top, 1), top - 1)
    down_w = complete({top: down_top})
    far = {key: v for key, v in down_w.items() if key & top}

    sums = []
    for piece in range(2):
        own, to_x, to_y, keep_x, keep_y = parts
        from_x, from_y = req(to_x, key_x), req(to_y, key_y)
        late_y = (keep_y + from_x[half:].astype(jnp.float32)).astype(jnp.bfloat16)
        late_x = (keep_x + from_y[half:].astype(jnp.float32)).astype(jnp.bfloat16)
        if piece == 0:
            far, late_x, late_y = tie((far, late_x, late_y))
            parts = down(place, acts, *gather(single(far), top, 1), top - 1)
        late_y, late_x = req(late_y, key_y), req(late_x, key_x)
        if piece == 0:
            parts, late_y, late_x = tie((parts, late_y, late_x))
        sums.append([own, from_x, from_y, late_x, late_y])
    return finish(upper, resid, sums)


def solution(mesh):
    in_specs = (
        P("req", "mlp"),
        P(None, "req", "mlp"),
        P(None, "req", "mlp"),
        P(("req", "mlp"), None),
        P(),
        P(),
        P(),
        P("mlp", None),
        P("req", "mlp"),
        P("req", "mlp"),
        P("req", "mlp"),
        P("req", None),
        P("req"),
        P(),
    )
    out_specs = P(("req", "mlp"), None)
    return jax.shard_map(
        per_device, mesh=mesh, in_specs=in_specs, out_specs=out_specs, check_vma=False
    )
```

```python
import functools
import math

import jax
import jax.numpy as jnp
from jax import lax
from jax.experimental import pallas as pl
from jax.experimental.pallas import tpu as pltpu
from jax.sharding import PartitionSpec as P

HD = 128
PB = 64
PLEN = 512
BPG = 8
PARTNERS = (0, 1, 4, 5)
GROUP = len(PARTNERS)
VMEM_LIMIT = 48 * 1024 * 1024
SHORT = pl.CostEstimate(flops=1024, bytes_accessed=1024, transcendentals=0)


EPSILON = 1e-06
THETA = 1000000.0


def rotation(positions):
    half_width = HD // 2
    exponent = jnp.arange(half_width, dtype=jnp.float32) * (2.0 / HD)
    inv_freq = jnp.power(jnp.float32(THETA), -exponent)
    angles = positions.astype(jnp.float32)[:, None] * inv_freq[None, :]
    cosine, sine = jnp.cos(angles), jnp.sin(angles)
    return jnp.concatenate([cosine, cosine], axis=1), jnp.concatenate([-sine, sine], axis=1)


def slot_layout(row_lengths, tok_count):
    req_ends = jnp.cumsum(row_lengths)
    starts = req_ends - row_lengths
    slot_ids = jnp.arange(tok_count, dtype=jnp.int32)
    request = jnp.sum((slot_ids[:, None] >= req_ends[None, :]).astype(jnp.int32), axis=1)
    member = request[:, None] == jnp.arange(row_lengths.shape[0], dtype=jnp.int32)[None, :]
    offset = slot_ids - jnp.sum(jnp.where(member, starts[None, :], 0), axis=1)
    return (request, offset)


def dot_rows(left, right):
    return lax.dot_general(
        left, right, (((1,), (1,)), ((), ())), preferred_element_type=jnp.float32
    )


def attention_kernel(
    start_ref, cos_ref, sin_ref, q_gain, k_gain, q_ref, k_ref, v_ref, pk_ref, pv_ref, out_ref, bias
):
    tok_count = k_ref.shape[1]
    tile = min(256, tok_count)
    scale = math.log2(math.e) / math.sqrt(HD)

    @pl.when(pl.program_id(0) == 0)
    def _():
        keys = lax.broadcasted_iota(jnp.int32, (tok_count, tok_count), 1)
        slots = lax.broadcasted_iota(jnp.int32, (tok_count, tok_count), 0)
        seen = (keys >= start_ref[...]) & (keys <= slots)
        bias[...] = jnp.where(seen, 0.0, -1e30)

    def prepare(values, gain, rows):
        values = values.astype(jnp.float32)
        mean_sq = jnp.mean(values * values, axis=-1, keepdims=True)
        scaled = values * lax.rsqrt(mean_sq + EPSILON) * gain[...]
        turned = scaled * cos_ref[rows, :] + pltpu.roll(scaled, HD // 2, 1) * sin_ref[rows, :]
        return turned.astype(jnp.bfloat16)

    key = prepare(k_ref[0], k_gain, pl.ds(0, tok_count))
    value = v_ref[0]
    pre_key = pk_ref[...].reshape(-1, HD)
    pre_value = pv_ref[...].reshape(-1, HD)
    for head in range(q_ref.shape[1] // HD):
        lanes = pl.ds(head * HD, HD)
        for first in range(0, tok_count, tile):
            rows = pl.ds(first, tile)
            last = first + tile
            query = prepare(q_ref[rows, lanes], q_gain, rows)
            pre_w = jnp.exp2(dot_rows(query, pre_key) * scale)
            suf_w = jnp.exp2(dot_rows(query, key[:last]) * scale + bias[rows, :last])
            total = jnp.sum(pre_w, axis=-1, keepdims=True) + jnp.sum(suf_w, axis=-1, keepdims=True)
            top = jnp.dot(
                pre_w.astype(jnp.bfloat16), pre_value, preferred_element_type=jnp.float32
            ) + jnp.dot(
                suf_w.astype(jnp.bfloat16), value[:last], preferred_element_type=jnp.float32
            )
            out_ref[rows, lanes] = (top / total).astype(out_ref.dtype)


def attention(start, cosine, sine, q_gain, k_gain, q_in, kv_in, chosen, first, count):
    tok_count = q_in.shape[0]
    groups = kv_in.shape[2] // HD
    width = q_in.shape[1] // groups
    blocks = chosen.shape[0]

    def same(rows, columns):
        return pl.BlockSpec((rows, columns), lambda g: (0, 0))

    def suffix(which):
        return pl.BlockSpec((1, tok_count, HD), lambda g: (which, 0, g + first))

    def prefix(which):
        return pl.BlockSpec((blocks, 1, PB, HD), lambda g: (0, which, 0, g + first))

    keys = tok_count + PLEN
    return pl.pallas_call(
        attention_kernel,
        grid=(count,),
        in_specs=[
            same(tok_count, 1),
            same(tok_count, HD),
            same(tok_count, HD),
            same(1, HD),
            same(1, HD),
            pl.BlockSpec((tok_count, width), lambda g: (0, g + first)),
            suffix(0),
            suffix(1),
            prefix(0),
            prefix(1),
        ],
        out_specs=pl.BlockSpec((tok_count, width), lambda g: (0, g)),
        out_shape=jax.ShapeDtypeStruct((tok_count, count * width), jnp.bfloat16),
        scratch_shapes=[pltpu.VMEM((tok_count, tok_count), jnp.float32)],
        compiler_params=pltpu.CompilerParams(vmem_limit_bytes=VMEM_LIMIT),
        cost_estimate=SHORT,
        name="attention",
    )(start, cosine, sine, q_gain, k_gain, q_in, kv_in, kv_in, chosen, chosen)


def project_kernel(core, *refs, n_parts, n_mlp):
    parts, weights, outs = refs[:n_parts], refs[n_parts : 2 * n_parts], refs[2 * n_parts :]
    rows = outs[0].shape[0]
    for k in range(n_mlp - 1, -1, -1):
        part = pl.ds(pl.multiple_of((core[0] ^ k) * rows, rows), rows)
        total = 0.0
        for x, w in zip(parts, weights):
            total = total + jnp.dot(x[part, :], w[...], preferred_element_type=jnp.float32)
        outs[k][...] = total.astype(outs[k].dtype)


def project(core, parts, w_out, n_mlp):
    tok_count, depth = parts[0].shape
    columns = w_out.shape[1]
    rows, tile = tok_count // n_mlp, 512
    n_parts = len(parts)
    return pl.pallas_call(
        functools.partial(project_kernel, n_parts=n_parts, n_mlp=n_mlp),
        grid_spec=pltpu.PrefetchScalarGridSpec(
            num_scalar_prefetch=1,
            grid=(columns // tile,),
            in_specs=[pl.BlockSpec((tok_count, depth), lambda n, core: (0, 0))] * n_parts
            + [
                pl.BlockSpec((depth, tile), functools.partial(lambda i, n, core: (i, n), i))
                for i in range(n_parts)
            ],
            out_specs=[pl.BlockSpec((rows, tile), lambda n, core: (0, n))] * n_mlp,
        ),
        out_shape=[
            jax.ShapeDtypeStruct((rows, columns), jnp.bfloat16 if k else jnp.float32)
            for k in range(n_mlp)
        ],
        compiler_params=pltpu.CompilerParams(vmem_limit_bytes=VMEM_LIMIT),
        cost_estimate=SHORT,
        name="project",
    )(core, *parts, *[w_out] * n_parts)


def normalize_kernel(hidden, gain, own, *refs):
    parts, (resid_ref, low_ref, high_ref) = refs[:-3], refs[-3:]
    step, middle = pl.program_id(0), pl.num_programs(0) // 2
    total = hidden[...].astype(jnp.float32) + own[...]
    for part in parts:
        total = total + part[...].astype(jnp.float32)
    resid = total.astype(resid_ref.dtype)
    resid_ref[...] = resid
    values = resid.astype(jnp.float32)
    mean_sq = jnp.mean(values * values, axis=-1, keepdims=True)
    normed = (values * lax.rsqrt(mean_sq + EPSILON) * gain[...]).astype(low_ref.dtype)

    @pl.when(step < middle)
    def _():
        low_ref[...] = normed

    @pl.when(step >= middle)
    def _():
        high_ref[...] = normed


def normalize(hidden, gain, own, parts):
    rows, columns = hidden.shape
    tile = min(64, rows // 2)
    middle = rows // 2 // tile
    spec = pl.BlockSpec((tile, columns), lambda i: (i, 0))
    low = pl.BlockSpec((tile, columns), lambda i: (jnp.minimum(i, middle - 1), 0))
    high = pl.BlockSpec((tile, columns), lambda i: (jnp.maximum(i - middle, 0), 0))
    halves = jax.ShapeDtypeStruct((rows // 2, columns), hidden.dtype)
    return pl.pallas_call(
        normalize_kernel,
        grid=(2 * middle,),
        in_specs=[spec, pl.BlockSpec((1, columns), lambda i: (0, 0)), spec] + [spec] * len(parts),
        out_specs=[spec, low, high],
        out_shape=[jax.ShapeDtypeStruct(hidden.shape, hidden.dtype), halves, halves],
        compiler_params=pltpu.CompilerParams(vmem_limit_bytes=VMEM_LIMIT),
        cost_estimate=SHORT,
        name="normalize",
    )(hidden, gain, own, *parts)


def move_kernel(scalar, *refs, n_in, plan):
    sems = refs[-1]
    copies = [
        pltpu.make_async_copy(src, dst, sems.at[i])
        for i, (src, dst) in enumerate(plan(scalar[0], refs[:n_in], refs[n_in:-1]))
    ]
    for copy in copies:
        copy.start()
    for copy in copies:
        copy.wait()


def move(scalar, arrays, shapes, plan, n_copies, name):
    anywhere = pl.BlockSpec(memory_space=pl.ANY)
    return pl.pallas_call(
        functools.partial(move_kernel, n_in=len(arrays), plan=plan),
        in_specs=[pl.BlockSpec(memory_space=pltpu.SMEM)] + [anywhere] * len(arrays),
        out_specs=[pl.BlockSpec(memory_space=pltpu.VMEM)] * len(shapes),
        out_shape=[jax.ShapeDtypeStruct(shape, jnp.bfloat16) for shape in shapes],
        scratch_shapes=[pltpu.SemaphoreType.DMA((n_copies,))],
        compiler_params=pltpu.CompilerParams(vmem_limit_bytes=VMEM_LIMIT),
        cost_estimate=SHORT,
        name=name,
    )(scalar, *arrays)


def cut(seat, blocks):
    rows, columns = blocks[0].shape
    width = columns // GROUP
    if width % 128:
        return [
            jnp.stack(
                [lax.dynamic_slice_in_dim(x, (seat[0] ^ j) * width, width, 1) for x in blocks]
            )
            for j in range(GROUP)
        ]

    def plan(seat, sources, targets):
        return [
            (source.at[:, pl.ds(pl.multiple_of((seat ^ j) * width, 128), width)], targets[j].at[m])
            for j in range(GROUP)
            for m, source in enumerate(sources)
        ]

    shapes = [(len(blocks), rows, width)] * GROUP
    return move(seat, blocks, shapes, plan, GROUP * len(blocks), "cut")


def merge(seat, parts):
    n_mats, rows, width = parts[0].shape
    if width % 128:
        return jnp.stack(parts, axis=1)

    def plan(_, sources, targets):
        return [
            (source.at[m], targets[0].at[m, j])
            for j, source in enumerate(sources)
            for m in range(n_mats)
        ]

    shapes = [(n_mats, GROUP, rows, width)]
    return move(seat, parts, shapes, plan, GROUP * n_mats, "merge")[0]


def weight_copies(me, refs, keys, matrix, target, mask, sems):
    copies = []
    for i, ref in enumerate(refs):
        part, entry = divmod(i, len(keys))
        rows, width = ref.shape[-2:]
        packed = len(target.shape) == 2
        lanes = pl.ds(part * width, width)
        if keys[entry] is None:
            place = target.at[:, lanes] if packed else target.at[part]
            copies.append(pltpu.make_async_copy(ref.at[matrix], place, sems.at[len(copies)]))
            continue
        for k, key in enumerate(keys[entry]):
            for j, partner in enumerate(PARTNERS):
                source = (me ^ (key ^ partner)) & mask
                here = pl.ds(pl.multiple_of(source * rows, 8), rows)
                place = target.at[here, lanes] if packed else target.at[part, here]
                copies.append(pltpu.make_async_copy(ref.at[matrix * len(keys[entry]) + k, j], place, sems.at[len(copies)]))
    return copies


def expand_kernel(me, *refs, n_parts, keys):
    n_weights = n_parts * len(keys)
    x_refs, refs = refs[: 2 * GROUP], refs[2 * GROUP :]
    w_refs, outs, refs = refs[:n_weights], refs[n_weights : n_weights + n_parts], refs[n_weights + n_parts :]
    x_all, gate_w, up_w, opened, x_sems, gate_sems, up_sems = refs
    width = outs[0].shape[1]
    half, depth = x_refs[0].shape
    rows = 4 * half
    places = [x_all.at[i // 4, pl.ds(i % 4 * half, half)] for i in range(2 * GROUP)]
    first = weight_copies(me[0], w_refs, keys, 0, gate_w, -1, gate_sems)
    first += [
        pltpu.make_async_copy(x_ref, place, x_sems.at[i])
        for i, (x_ref, place) in enumerate(zip(x_refs, places))
    ]
    second = weight_copies(me[0], w_refs, keys, 1, up_w, -1, up_sems)
    for copy in first + second:
        copy.start()

    def product(x, weight):
        if len(weight.shape) == 2:
            whole = jnp.dot(x, weight[...], preferred_element_type=jnp.float32)
            return [whole[:, part * width : (part + 1) * width] for part in range(n_parts)]
        return [
            jnp.dot(x, weight[part], preferred_element_type=jnp.float32) for part in range(n_parts)
        ]

    def gate_step(i, carry):
        for part, gate in enumerate(product(x_all[i], gate_w)):
            opened[i, part] = gate / (1.0 + jnp.exp(-gate))
        return carry

    def up_step(i, carry):
        lines = pl.ds(pl.multiple_of(i * rows, rows), rows)
        for part, upward in enumerate(product(x_all[i], up_w)):
            outs[part][lines, :] = (opened[i, part] * upward).astype(outs[part].dtype)
        return carry

    for copy in first:
        copy.wait()
    lax.fori_loop(0, GROUP // 2, gate_step, 0)
    for copy in second:
        copy.wait()
    lax.fori_loop(0, GROUP // 2, up_step, 0)


def expand(me, normed, keys, weights):
    rows, depth = 2 * normed[0].shape[0], normed[0].shape[1]
    n_parts = len(weights)
    width = weights[0][0].shape[-1]
    total = rows * GROUP
    n_copies = n_parts * GROUP * sum(len(entry or (0,)) for entry in keys)
    shape = (depth, n_parts * width) if width % 128 == 0 else (n_parts, depth, width)
    vmem, anywhere = pl.BlockSpec(memory_space=pltpu.VMEM), pl.BlockSpec(memory_space=pl.ANY)
    return pl.pallas_call(
        functools.partial(expand_kernel, n_parts=n_parts, keys=keys),
        in_specs=[pl.BlockSpec(memory_space=pltpu.SMEM)]
        + [anywhere] * (len(normed) + n_parts * len(keys)),
        out_specs=[vmem] * n_parts,
        out_shape=[jax.ShapeDtypeStruct((total, width), jnp.bfloat16)] * n_parts,
        scratch_shapes=[
            pltpu.VMEM((GROUP // 2, 2 * rows, depth), jnp.bfloat16),
            pltpu.VMEM(shape, jnp.bfloat16),
            pltpu.VMEM(shape, jnp.bfloat16),
            pltpu.VMEM((GROUP // 2, n_parts, 2 * rows, width), jnp.float32),
            pltpu.SemaphoreType.DMA((len(normed),)),
            pltpu.SemaphoreType.DMA((n_copies,)),
            pltpu.SemaphoreType.DMA((n_copies,)),
        ],
        compiler_params=pltpu.CompilerParams(vmem_limit_bytes=VMEM_LIMIT),
        cost_estimate=SHORT,
        name="gate_up",
    )(me, *normed, *[array for part in weights for array in part])


def down_kernel(me, *refs, n_parts, keys, mask):
    n_weights = n_parts * len(keys)
    act_refs, w_refs = refs[:n_parts], refs[n_parts : n_parts + n_weights]
    own, to_x, to_y, keep_x, keep_y, acts, weight, a_sems, w_sems = refs[n_parts + n_weights :]
    width = act_refs[0].shape[1]
    rows = own.shape[0]
    half = rows // 2
    packed = len(acts.shape) == 2
    copies = weight_copies(me[0], w_refs, keys, 0, weight, mask, w_sems)
    for i in range(n_parts):
        place = acts.at[:, pl.ds(i * width, width)] if packed else acts.at[i]
        copies.append(pltpu.make_async_copy(act_refs[i], place, a_sems.at[i]))
    for copy in copies:
        copy.start()
    for copy in copies:
        copy.wait()

    def sums(block):
        here = pl.ds(block * rows, 2 * rows)
        if packed:
            total = dot_rows(acts[here, :], weight[...])
        else:
            total = sum(dot_rows(acts[i, here, :], weight[i]) for i in range(n_parts))
        return total[:rows], total[rows:]

    near, far = sums(2)
    to_x[half:, :] = far[:half].astype(jnp.bfloat16)
    to_y[half:, :] = far[half:].astype(jnp.bfloat16)
    to_y[:half, :] = near[half:].astype(jnp.bfloat16)
    keep_y[...] = near[:half]
    near, far = sums(0)
    to_x[:half, :] = far[:half].astype(jnp.bfloat16)
    keep_x[...] = far[half:]
    own[...] = near


def down(me, acts, keys, weights, mask):
    total, width = acts[0].shape
    n_parts = len(acts)
    columns = sum(math.prod(array.shape[:-1]) for array in weights[0])
    rows = total // GROUP
    if width % 128 == 0:
        shapes = [(total, n_parts * width), (columns, n_parts * width)]
    else:
        shapes = [(n_parts, total, width), (n_parts, columns, width)]
    outs = [(rows, jnp.float32), (rows, jnp.bfloat16), (rows, jnp.bfloat16)]
    outs += [(rows // 2, jnp.float32)] * 2
    return pl.pallas_call(
        functools.partial(down_kernel, n_parts=n_parts, keys=keys, mask=mask),
        out_shape=[jax.ShapeDtypeStruct((length, columns), dtype) for length, dtype in outs],
        in_specs=[pl.BlockSpec(memory_space=pltpu.SMEM)]
        + [pl.BlockSpec(memory_space=pl.ANY)] * (n_parts + n_parts * len(keys)),
        out_specs=[pl.BlockSpec(memory_space=pltpu.VMEM)] * 5,
        scratch_shapes=[pltpu.VMEM(shape, jnp.bfloat16) for shape in shapes]
        + [
            pltpu.SemaphoreType.DMA((n_parts,)),
            pltpu.SemaphoreType.DMA((n_parts * GROUP * sum(len(entry or (0,)) for entry in keys),)),
        ],
        compiler_params=pltpu.CompilerParams(vmem_limit_bytes=VMEM_LIMIT),
        cost_estimate=SHORT,
        name="down",
    )(me, *acts, *[array for part in weights for array in part])


def finish_kernel(place, resid, own, from_x, from_y, late_x, late_y, out_ref):
    half = resid.shape[0] // 2
    for rows, first, late in (
        (pl.ds(0, half), from_x, late_y),
        (pl.ds(half, half), from_y, late_x),
    ):
        total = resid[rows, :].astype(jnp.float32) + own[rows, :]
        total = total + first[:half, :].astype(jnp.float32) + late[...].astype(jnp.float32)
        out_ref[rows, :] = total.astype(out_ref.dtype)


def finish(place, out, parts):
    rows, width = out.shape[0], out.shape[1] // 2
    placed = pl.BlockSpec((rows, width), lambda i, place: (0, place[0]))
    specs = [pl.BlockSpec(part.shape, lambda i, place: (0, 0)) for part in parts]
    return pl.pallas_call(
        finish_kernel,
        grid_spec=pltpu.PrefetchScalarGridSpec(
            num_scalar_prefetch=1, grid=(1,), in_specs=[placed] + specs, out_specs=placed
        ),
        out_shape=jax.ShapeDtypeStruct(out.shape, out.dtype),
        input_output_aliases={1: 0},
        compiler_params=pltpu.CompilerParams(vmem_limit_bytes=VMEM_LIMIT),
        cost_estimate=SHORT,
        name="finish",
    )(place, out, *parts)


def swap(value, axis, size, bits):
    return lax.ppermute(value, axis, [(i, i ^ bits) for i in range(size)])


def per_device(
    q_in,
    kv_in,
    prefix_kv,
    hidden_in,
    q_gain,
    k_gain,
    post_gain,
    w_out,
    w_gate,
    w_up,
    w_down_t,
    lengths,
    row_group,
    owner_block,
):
    n_req, n_mlp = lax.axis_size("req"), lax.axis_size("mlp")
    me, core = lax.axis_index("req"), lax.axis_index("mlp")
    tok_count = q_in.shape[0]
    local_groups = kv_in.shape[2] // HD

    def tie(tree):
        leaves, shape = jax.tree.flatten(tree)
        fixed = [isinstance(leaf, int) for leaf in leaves]
        held = iter(lax.optimization_barrier([x for x, f in zip(leaves, fixed) if not f]))
        return jax.tree.unflatten(shape, [x if f else next(held) for x, f in zip(leaves, fixed)])

    top = n_req // 2
    others = [1 << i for i in range(n_req.bit_length()) if 1 << i < n_req and 1 << i not in PARTNERS]
    others = others[::-1]
    seat = ((me & 1) + (me >> 2 & 1) * 2)[None]
    place, upper = me[None], (me // top)[None]

    def req(value, key):
        return swap(value, "req", n_req, key)

    def cores(part):
        return [part] + [swap(part, "mlp", n_mlp, k) for k in range(1, n_mlp)]

    def trade(parts):
        return [parts[0]] + [req(part, key) for part, key in zip(parts[1:], PARTNERS[1:])]

    def complete(arrays):
        for key in others[1:]:
            for held_key in list(arrays):
                if held_key ^ key not in arrays:
                    arrays[held_key ^ key] = req(arrays[held_key], key)
        return arrays

    def single(arrays):
        return [([key], cores(array)) for key, array in arrays.items()]

    def gather(shares, count, n_mats):
        keys, parts = [keys for keys, _ in shares], list(zip(*[parts for _, parts in shares]))
        if parts[0][0].shape[2] % 16 == 0:
            return keys, [list(part) for part in parts]
        spots = [(key ^ partner) % count for entry in keys for key in entry for partner in PARTNERS]
        spots = jnp.asarray([spots.index(i) for i in range(count)])
        spots = spots[(me ^ jnp.arange(count)) % count]
        ordered = []
        for part in parts:
            width = part[0].shape[-1]
            whole = [x.reshape(n_mats, -1, *x.shape[2:]) for x in part]
            whole = jnp.take(jnp.concatenate(whole, axis=1), spots, axis=1)
            ordered.append([whole.reshape(n_mats, -1, width)])
        return [None], ordered

    planes = [prefix_kv] + [req(prefix_kv, 4 * k) for k in range(1, n_req // 4)]
    held = jnp.stack(planes)
    slot = jnp.argsort(owner_block) ^ me
    spot = slot // 4 + slot % 4 * (n_req // 4)
    picked = lax.dynamic_slice_in_dim(spot, row_group[0] * BPG, BPG, 0)

    parts = list(cut(seat, [w_gate, w_up]))
    held, parts[3] = tie((held, parts[3]))
    open_w = merge(seat, trade(parts))
    open_w, w_down_t = tie((open_w, w_down_t))
    last = others[-1]
    held = jnp.stack([held] + [req(held, k) for k in range(1, 4)])
    held = held.reshape(n_req, 2, PB, local_groups * HD)
    chosen = jnp.take(held, picked, axis=0)
    open_top, open_last = req(open_w, top), req(open_w, last)

    _, offset = slot_layout(lengths[0], tok_count)
    cosine, sine = rotation(offset + PLEN)
    start = (jnp.arange(tok_count, dtype=jnp.int32) - offset)[:, None]
    gains = q_gain[None], k_gain[None]

    chosen, cosine, sine, start = tie((chosen, cosine, sine, start))
    attn = attention(start, cosine, sine, *gains, q_in, kv_in, chosen, 0, local_groups)
    attn, down_parts = tie((attn, trade(cut(seat, [w_down_t]))))
    down_own = merge(seat, down_parts)
    down_last = req(down_own, last)

    own_rows = hidden_in.shape[0]
    sums = project(core[None], [attn], w_out, n_mlp)
    parts = [swap(sums[k], "mlp", n_mlp, k) for k in range(1, n_mlp)]
    resid, *own_normed = normalize(hidden_in, post_gain[None], sums[0], parts)

    own_normed, open_top, open_last, down_own, down_last = tie(
        (own_normed, open_top, open_last, down_own, down_last)
    )

    half = own_rows // 2
    key_x, key_y = PARTNERS[1:3]
    low, high = own_normed
    low_x, high_y = req(low, key_x), req(high, key_y)
    late = complete({0: open_w, last: open_last, top: open_top})
    late = {key: late[key] for key in late if key not in (0, last, top)}
    open_all = single({0: open_w})
    low_x, high_y = tie((low_x, high_y))
    high_x, low_y = req(high, key_x), req(low, key_y)
    diag = [req(low_x, key_y), req(high_y, key_x)]
    open_all = open_all + single({last: open_last, top: open_top})
    diag, high_x, low_y, open_all, late, down_own, down_last = tie(
        (diag, high_x, low_y, open_all, late, down_own, down_last)
    )
    open_all = open_all + single(late)
    normed = [low, high, low_x, high_x, low_y, high_y] + diag

    acts = expand(place, normed, *gather(open_all, n_req, 2))
    down_top = req(down_own, top)
    near = single({0: down_own, last: down_last})
    acts, near = tie((acts, near))
    down_w = complete({0: down_own, last: down_last}) if n_req > 16 else {}
    near = near + single({key: v for key, v in down_w.items() if key not in (0, last)})
    parts = down(place, acts, *gather(near, top, 1), top - 1)
    down_w = complete({top: down_top})
    far = {key: v for key, v in down_w.items() if key & top}

    out = resid
    for piece in range(2):
        own, to_x, to_y, keep_x, keep_y = parts
        from_x, from_y = req(to_x, key_x), req(to_y, key_y)
        if piece == 1:
            out, from_x, from_y = tie((out, from_x, from_y))
        late_y = (keep_y + from_x[half:].astype(jnp.float32)).astype(jnp.bfloat16)
        late_x = (keep_x + from_y[half:].astype(jnp.float32)).astype(jnp.bfloat16)
        if piece == 0:
            far, late_x, late_y = tie((far, late_x, late_y))
            parts = down(place, acts, *gather(single(far), top, 1), top - 1)
        late_y, late_x = req(late_y, key_y), req(late_x, key_x)
        if piece == 0:
            parts, late_y, late_x = tie((parts, late_y, late_x))
        out = finish(upper ^ piece, out, [own, from_x, from_y, late_x, late_y])
    return out


def solution(mesh):
    in_specs = (
        P("req", "mlp"),
        P(None, "req", "mlp"),
        P(None, "req", "mlp"),
        P(("req", "mlp"), None),
        P(),
        P(),
        P(),
        P("mlp", None),
        P("req", "mlp"),
        P("req", "mlp"),
        P("req", "mlp"),
        P("req", None),
        P("req"),
        P(),
    )
    out_specs = P(("req", "mlp"), None)
    return jax.shard_map(
        per_device, mesh=mesh, in_specs=in_specs, out_specs=out_specs, check_vma=False
    )
```
